32 devices in a mesh: groups: 2 (over y), tm: 4 (over x, core), space: 4 (over z).
Axes of the slice: x: 2, y: 2, z: 4, core: 2. Of those that a mesh axis runs over, the one named last changes fastest.
Arguments:
- query: bfloat16 [8192, 1536], P(('groups', 'tm', 'space')), parts along dimension 0, may hold values from -24 to 24
- key_in: bfloat16 [8192, 1536], P(('groups', 'tm', 'space')), parts along dimension 0, may hold values from -24 to 24
- value_in: bfloat16 [8192, 1536], P(('groups', 'tm', 'space')), parts along dimension 0, may hold values from -12 to 12
- grad_out: bfloat16 [8192, 1536], P(('groups', 'tm', 'space')), parts along dimension 0, may hold values from -48 to 48
- frame_ids: int32 [8192], P(('groups', 'tm', 'space')), parts along dimension 0, may hold values from 0 to 15, as said below
- time_ids: int32 [8192], P(('groups', 'tm', 'space')), parts along dimension 0, may hold values from 0 to 3, as said below
- tile_valid: int32 [8, 4], P(('groups', 'tm'), 'space'), parts along dimension 0, may hold values from 128 to 256
Outputs:
- query_grad: bfloat16 [8192, 1536], P(('groups', 'tm', 'space')), parts along dimension 0
- key_grad: bfloat16 [8192, 1536], P(('groups', 'tm', 'space')), parts along dimension 0
- value_grad: bfloat16 [8192, 1536], P(('groups', 'tm', 'space')), parts along dimension 0
The draws below stay inside these ranges and needn't reach their ends.
There are 2 independent parts, one for each index of `groups`. The reference program is written for one: setup_inputs(seed, part) draws one part's arguments, and reference() takes and returns one part's arrays. A program takes and returns all parts, laid end to end along the dimension named above; each array names one. Nothing has to cross between parts.
Inputs may be any that keep to these rules, and one draw needn't show every extreme that they name: `frame_ids`: in every block the first 16 rows carry the ids 0 to 15 in order. `time_ids`: in every block the first 4 rows carry the ids 0 to 3 in order.
All inputs are finite; a program needn't handle non-finite values.
Results may differ from the reference program's by a relative error of at most 0.0072.
Values may be sent and summed in bfloat16 or wider, within the bound.
No kernel may reach another device: no remote copies, remote signals or barrier semaphores. Data moves between devices by JAX's collectives and lax.ppermute only.
A program may use at most 64 MiB of HBM per device.

```python
from functools import partial
import jax
import jax.numpy as jnp
from jax import lax

H = 12
HD = 128
WIN = 64
WIN_FRAME = 4
KF = 16
KT = 4
T_DEV = 256
TOKENS = 4096
N_TM = 4
N_SPACE = 4


def time_layout(key):
    ids_key = jax.random.fold_in(key, 129)
    labels = jax.random.randint(ids_key, (TOKENS,), 0, KT, dtype=jnp.int32)
    within = jnp.arange(TOKENS, dtype=jnp.int32) % T_DEV
    return jnp.where(within < KT, within, labels)


def block_places():
    block_of = jnp.arange(TOKENS, dtype=jnp.int32) // T_DEV
    return (block_of, block_of // N_SPACE)


def segment_offsets(key, labels):
    block_of, stretch_of = block_places()
    common = jnp.clip(0.775 * jax.random.normal(jax.random.fold_in(key, 1), (N_TM, KT, H * HD), jnp.float32), -3.0, 3.0)
    local_part = jnp.clip(0.63 * jax.random.normal(jax.random.fold_in(key, 2), (N_TM * N_SPACE, KT, H * HD), jnp.float32), -3.0, 3.0)
    return common[stretch_of, labels] + local_part[block_of, labels]


def shared_offsets(key):
    labels = time_layout(key)
    return segment_offsets(jax.random.fold_in(key, 201), labels)


def draw_query(key, part):
    offsets = shared_offsets(key)
    key = jax.random.fold_in(key, 11)
    values_drawn = jnp.clip(jax.random.normal(key, (TOKENS, H * HD), jnp.float32), -6.0, 6.0) + 0.35 * offsets
    return values_drawn.astype(jnp.bfloat16)


def draw_key_in(key, part):
    offsets = shared_offsets(key)
    key = jax.random.fold_in(key, 13)
    values_drawn = jnp.clip(jax.random.normal(key, (TOKENS, H * HD), jnp.float32), -6.0, 6.0) + offsets
    return values_drawn.astype(jnp.bfloat16)


def draw_value_in(key, part):
    labels = time_layout(key)
    key = jax.random.fold_in(key, 19)
    offsets = segment_offsets(jax.random.fold_in(key, 3), labels)
    values_drawn = jnp.clip(jax.random.normal(key, (TOKENS, H * HD), jnp.float32), -6.0, 6.0) + offsets
    return values_drawn.astype(jnp.bfloat16)


def draw_grad_out(key, part):
    labels = time_layout(key)
    key = jax.random.fold_in(key, 17)
    block_of, stretch_of = block_places()
    trend = jnp.clip(0.7 * jax.random.normal(jax.random.fold_in(key, 3), (N_TM, KT, H * HD), jnp.float32), -2.0, 2.0)
    noise = jnp.clip(jax.random.normal(key, (TOKENS, H * HD), jnp.float32), -4.0, 4.0)
    values_drawn = 8.0 * (noise + trend[stretch_of, labels])
    return values_drawn.astype(jnp.bfloat16)


def draw_frame_ids(key, part):
    key = jax.random.fold_in(key, 23)
    labels = jax.random.randint(key, (TOKENS,), 0, KF, dtype=jnp.int32)
    within = jnp.arange(TOKENS, dtype=jnp.int32) % T_DEV
    return jnp.where(within < KF, within, labels)


def draw_time_ids(key, part):
    return time_layout(key)


def draw_tile_valid(key, part):
    key = jax.random.fold_in(key, 37)
    tile_span = WIN_FRAME * WIN
    values_drawn = jax.random.randint(key, (N_TM, N_SPACE), tile_span // 2, tile_span + 1, dtype=jnp.int32)
    chosen = jax.random.randint(jax.random.fold_in(key, 5), (), 0, N_TM * N_SPACE, dtype=jnp.int32)
    places = jnp.arange(N_TM * N_SPACE, dtype=jnp.int32).reshape(N_TM, N_SPACE)
    return jnp.where(places == chosen, tile_span, values_drawn)


def setup_inputs(seed: int = 0, part: int = 0) -> dict:
    keys = jax.random.split(jax.random.key(seed), 8)
    part_keys = jax.random.split(jax.random.fold_in(keys[7], part), 8)
    return {
        "query": draw_query(jax.random.fold_in(jax.random.fold_in(keys[7], part), 71), part),
        "key_in": draw_key_in(jax.random.fold_in(jax.random.fold_in(keys[7], part), 71), part),
        "value_in": draw_value_in(jax.random.fold_in(jax.random.fold_in(keys[7], part), 71), part),
        "grad_out": draw_grad_out(jax.random.fold_in(jax.random.fold_in(keys[7], part), 71), part),
        "frame_ids": draw_frame_ids(jax.random.fold_in(jax.random.fold_in(keys[7], part), 71), part),
        "time_ids": draw_time_ids(jax.random.fold_in(jax.random.fold_in(keys[7], part), 71), part),
        "tile_valid": draw_tile_valid(jax.random.fold_in(jax.random.fold_in(keys[7], part), 71), part),
    }


MASK_FILL = -1e30


def member_table(labels_in, live_rows, groups):
    labels = jnp.arange(groups, dtype=jnp.int32)
    return (labels_in[:, None] == labels[None, :]) & live_rows[:, None]


def pool_block(labels_in, live_rows, keys_in, values_in, groups):
    member = member_table(labels_in, live_rows, groups)
    table = member.astype(jnp.bfloat16)
    counts = jnp.sum(member.astype(jnp.float32), axis=0)
    sums_k = jnp.dot(table.T, keys_in, preferred_element_type=jnp.float32)
    sums_v = jnp.dot(table.T, values_in, preferred_element_type=jnp.float32)
    return (sums_k / counts[:, None]).astype(jnp.bfloat16), (sums_v / counts[:, None]).astype(jnp.bfloat16), counts


def attend(query, key_in, value_in, masked_grad, live_rows, coarse_k, coarse_v):
    length, features = query.shape
    windows = length // WIN
    head_count = features // HD
    factor = HD ** -0.5
    query_heads = query.reshape(windows, WIN, head_count, HD).astype(jnp.float32)
    key_heads = key_in.reshape(windows, WIN, head_count, HD).astype(jnp.float32)
    value_heads = value_in.reshape(windows, WIN, head_count, HD).astype(jnp.float32)
    grad_heads = masked_grad.reshape(windows, WIN, head_count, HD).astype(jnp.float32)
    coarse_kh = coarse_k.reshape(-1, head_count, HD).astype(jnp.float32)
    coarse_vh = coarse_v.reshape(-1, head_count, HD).astype(jnp.float32)
    window_score = jnp.einsum('wqhd,wkhd->wqhk', query_heads, key_heads) * factor
    window_score = jnp.where(live_rows.reshape(windows, 1, 1, WIN), window_score, MASK_FILL)
    coarse_score = jnp.einsum('wqhd,khd->wqhk', query_heads, coarse_kh) * factor
    row_max = jnp.maximum(jnp.max(window_score, axis=-1), jnp.max(coarse_score, axis=-1))[..., None]
    window_exp = jnp.exp(window_score - row_max)
    coarse_exp = jnp.exp(coarse_score - row_max)
    row_sum = (jnp.sum(window_exp, axis=-1) + jnp.sum(coarse_exp, axis=-1))[..., None]
    window_weight = window_exp / row_sum
    coarse_weight = coarse_exp / row_sum
    window_wb = window_weight.astype(jnp.bfloat16)
    coarse_wb = coarse_weight.astype(jnp.bfloat16)
    attended = jnp.einsum('wqhk,wkhd->wqhd', window_wb.astype(jnp.float32), value_heads)
    attended = attended + jnp.einsum('wqhk,khd->wqhd', coarse_wb.astype(jnp.float32), coarse_vh)
    delta = jnp.sum(grad_heads * attended, axis=-1, keepdims=True)
    window_dp = jnp.einsum('wqhd,wkhd->wqhk', grad_heads, value_heads)
    coarse_dp = jnp.einsum('wqhd,khd->wqhk', grad_heads, coarse_vh)
    window_ds = (factor * window_weight * (window_dp - delta)).astype(jnp.bfloat16)
    coarse_ds = (factor * coarse_weight * (coarse_dp - delta)).astype(jnp.bfloat16)
    query_grad = jnp.einsum('wqhk,wkhd->wqhd', window_ds.astype(jnp.float32), key_heads)
    query_grad = query_grad + jnp.einsum('wqhk,khd->wqhd', coarse_ds.astype(jnp.float32), coarse_kh)
    window_kg = jnp.einsum('wqhk,wqhd->wkhd', window_ds.astype(jnp.float32), query_heads)
    window_vg = jnp.einsum('wqhk,wqhd->wkhd', window_wb.astype(jnp.float32), grad_heads)
    return (query_grad.reshape(length, features), window_kg.reshape(length, features),
            window_vg.reshape(length, features), coarse_ds, coarse_wb, query_heads, grad_heads)


def coarse_terms(coarse_ds, coarse_wb, query_heads, grad_heads, offset, amount):
    ds_part = lax.dynamic_slice_in_dim(coarse_ds, offset, amount, 3).astype(jnp.float32)
    wb_part = lax.dynamic_slice_in_dim(coarse_wb, offset, amount, 3).astype(jnp.float32)
    grad_k = jnp.einsum('wqhk,wqhd->khd', ds_part, query_heads)
    grad_v = jnp.einsum('wqhk,wqhd->khd', wb_part, grad_heads)
    return jnp.concatenate([grad_k.reshape(amount, -1), grad_v.reshape(amount, -1)], axis=1)


def spread(member, counts, grads):
    share = grads / counts[:, None]
    return jnp.dot(member.astype(jnp.float32), share, precision=lax.Precision.HIGHEST)


def reference(query, key_in, value_in, grad_out, frame_ids, time_ids, tile_valid):
    features = H * HD
    tile_span = WIN_FRAME * WIN
    blocks = N_TM * N_SPACE
    shape_four = (N_TM, N_SPACE, T_DEV, features)
    query_four = query.reshape(shape_four)
    key_four = key_in.reshape(shape_four)
    value_four = value_in.reshape(shape_four)
    grad_four = grad_out.reshape(shape_four)
    frame_four = frame_ids.reshape(N_TM, N_SPACE, T_DEV)
    time_four = time_ids.reshape(N_TM, N_SPACE, T_DEV)
    position = jnp.arange(T_DEV, dtype=jnp.int32) % tile_span
    live_four = position[None, None, :] < tile_valid[:, :, None]
    pool_frame = jax.vmap(jax.vmap(partial(pool_block, groups=KF)))
    pool_time = jax.vmap(jax.vmap(partial(pool_block, groups=KT)))
    frame_k, frame_v, frame_count = pool_frame(frame_four, live_four, key_four, value_four)
    time_k, time_v, time_count = pool_time(time_four, live_four, key_four, value_four)
    frame_rows = N_TM * KF
    time_rows = N_SPACE * KT

    def advance(totals, block_index):
        frame_acc, time_acc = totals
        frame_stretch = block_index // N_SPACE
        space_tile = block_index % N_SPACE
        coarse_k = jnp.concatenate([frame_k[:, space_tile].reshape(frame_rows, features),
                                    time_k[frame_stretch].reshape(time_rows, features)], axis=0)
        coarse_v = jnp.concatenate([frame_v[:, space_tile].reshape(frame_rows, features),
                                    time_v[frame_stretch].reshape(time_rows, features)], axis=0)
        live_rows = live_four[frame_stretch, space_tile]
        masked_grad = grad_four[frame_stretch, space_tile] * live_rows[:, None].astype(jnp.bfloat16)
        query_grad, window_kg, window_vg, coarse_ds, coarse_wb, query_heads, grad_heads = attend(
            query_four[frame_stretch, space_tile], key_four[frame_stretch, space_tile],
            value_four[frame_stretch, space_tile], masked_grad, live_rows, coarse_k, coarse_v)
        frame_term = coarse_terms(coarse_ds, coarse_wb, query_heads, grad_heads, 0, frame_rows)
        time_term = coarse_terms(coarse_ds, coarse_wb, query_heads, grad_heads, frame_rows, time_rows)
        frame_acc = frame_acc.at[:, space_tile].add(frame_term.reshape(N_TM, KF, 2 * features))
        time_acc = time_acc.at[frame_stretch].add(time_term.reshape(N_SPACE, KT, 2 * features))
        return (frame_acc, time_acc), (query_grad.astype(jnp.bfloat16), window_kg, window_vg)

    start_totals = (jnp.zeros((N_TM, N_SPACE, KF, 2 * features), jnp.float32),
                    jnp.zeros((N_TM, N_SPACE, KT, 2 * features), jnp.float32))
    (frame_acc, time_acc), (query_grad, window_kg, window_vg) = lax.scan(
        advance, start_totals, jnp.arange(blocks, dtype=jnp.int32))

    def finish(frame_lab, time_lab, live_rows, frame_cnt, time_cnt, frame_grad, time_grad, win_k, win_v):
        back = spread(member_table(frame_lab, live_rows, KF), frame_cnt, frame_grad)
        back = back + spread(member_table(time_lab, live_rows, KT), time_cnt, time_grad)
        return (win_k + back[:, :features]).astype(jnp.bfloat16), (win_v + back[:, features:]).astype(jnp.bfloat16)

    key_grad, value_grad = jax.vmap(jax.vmap(finish))(
        frame_four, time_four, live_four, frame_count, time_count, frame_acc, time_acc,
        window_kg.reshape(shape_four), window_vg.reshape(shape_four))
    return (query_grad.reshape(TOKENS, features), key_grad.reshape(TOKENS, features),
            value_grad.reshape(TOKENS, features))
```

```python
import functools
import math

import jax
import jax.numpy as jnp
from jax import lax
from jax.experimental import pallas as pl
from jax.experimental.pallas import tpu as pltpu
from jax.sharding import PartitionSpec as P

HD = 128
WIN = 64
WIN_FRAME = 4
KF = 16
KT = 4
PAIR = 2 * WIN
SPAN = WIN_FRAME * WIN

MASK_FILL = -1e30
FACTOR = HD ** (-0.5)
LIMIT = 24 * 1024 * 1024

VMEM = pl.BlockSpec(memory_space=pltpu.VMEM)
SMEM = pl.BlockSpec(memory_space=pltpu.SMEM)


def dot(a, b, dims):
    return lax.dot_general(a, b, (dims, ((), ())), preferred_element_type=jnp.float32)


NT = ((1,), (1,))
NN = ((1,), (0,))
TN = ((0,), (0,))


def call(kernel, outs, ins, flops, moved):
    return pl.pallas_call(
        kernel,
        out_shape=outs,
        in_specs=[SMEM if i.shape == (1, 1) else VMEM for i in ins],
        out_specs=[VMEM] * len(outs),
        compiler_params=pltpu.CompilerParams(vmem_limit_bytes=LIMIT),
        cost_estimate=pl.CostEstimate(
            flops=flops, bytes_accessed=moved, transcendentals=0
        ),
    )(*ins)


def member_rows(valid, frame, time, length):
    rows = KF + 8
    label = lax.broadcasted_iota(jnp.int32, (rows, length), 0)
    place = lax.broadcasted_iota(jnp.int32, (rows, length), 1) % SPAN
    ids = jnp.where(label < KF, frame, time + KF)
    return jnp.where((ids == label) & (place < valid), 1.0, 0.0)


def pool_kernel(valid_ref, frame_ref, time_ref, k_ref, v_ref, f_ref, t_ref):
    length, features = k_ref.shape
    member = member_rows(valid_ref[0, 0], frame_ref[...], time_ref[...], length)
    share = 1.0 / jnp.maximum(jnp.sum(member, axis=1, keepdims=True), 1.0)
    table = member.astype(jnp.bfloat16)
    for ref, at in ((k_ref, 0), (v_ref, features)):
        pooled = dot(table, ref[...], NN) * share
        f_ref[:, at : at + features] = pooled[:KF].astype(jnp.bfloat16)
        t_ref[:, at : at + features] = pooled[KF : KF + KT].astype(jnp.bfloat16)


def coarse_rows(refs, at):
    parts = [r[:, at : at + HD].astype(jnp.float32) for r in refs]
    return jnp.concatenate(parts, axis=0).astype(jnp.bfloat16)


def weigh_kernel(counts, valid_ref, q_ref, k_ref, v_ref, g_ref, *refs):
    coarse = refs[: counts[0]]
    outs = refs[counts[0] :]
    dsw_ref, ww_ref, dsc_ref = outs[:3]
    term_refs = outs[3:]
    length, features = q_ref.shape
    heads = features // HD
    valid = valid_ref[0, 0]
    live = lax.broadcasted_iota(jnp.int32, (length, HD), 0) % SPAN < valid
    lane = lax.broadcasted_iota(jnp.int32, (WIN, PAIR), 1)
    row = lax.broadcasted_iota(jnp.int32, (WIN, PAIR), 0)
    first = lane < WIN
    place = row + jnp.where(first, 0, WIN)
    scale = FACTOR * math.log2(math.e)
    for h in range(heads):
        at = h * HD
        kc = coarse_rows(coarse, at)
        vc = coarse_rows(coarse, features + at)
        q = q_ref[:, at : at + HD]
        g = jnp.where(live, g_ref[:, at : at + HD], 0)
        ds_parts, w_parts = [], []
        for p in range(length // PAIR):
            rows = slice(p * PAIR, (p + 1) * PAIR)
            keys = jnp.concatenate([k_ref[rows, at : at + HD], kc], axis=0)
            values = jnp.concatenate([v_ref[rows, at : at + HD], vc], axis=0)
            s = dot(keys, q[rows], NT)
            d = dot(values, g[rows], NT)
            sw = jnp.where(first, s[:WIN], s[WIN:PAIR])
            sw = jnp.where((place + p * PAIR) % SPAN < valid, sw, MASK_FILL)
            sc = s[PAIR:]
            dw = jnp.where(first, d[:WIN], d[WIN:PAIR])
            dc = d[PAIR:]
            top = jnp.maximum(
                jnp.max(sw, axis=0, keepdims=True), jnp.max(sc, axis=0, keepdims=True)
            )
            ew = jnp.exp2((sw - top) * scale)
            ec = jnp.exp2((sc - top) * scale)
            total = jnp.sum(ew, axis=0, keepdims=True) + jnp.sum(
                ec, axis=0, keepdims=True
            )
            inv = 1.0 / total
            ww = ew * inv
            wc = ec * inv
            delta = jnp.sum(ww * dw, axis=0, keepdims=True) + jnp.sum(
                wc * dc, axis=0, keepdims=True
            )
            dsw = (FACTOR * ww) * (dw - delta)
            dsc = (FACTOR * wc) * (dc - delta)
            lanes = slice(p * PAIR, (p + 1) * PAIR)
            dsw_ref[h, :, lanes] = dsw.astype(jnp.bfloat16)
            ww_ref[h, :, lanes] = ww.astype(jnp.bfloat16)
            ds_parts.append(dsc.astype(jnp.bfloat16))
            w_parts.append(wc.astype(jnp.bfloat16))
        dsc = jnp.concatenate(ds_parts, axis=1)
        wc = jnp.concatenate(w_parts, axis=1)
        dsc_ref[h] = dsc
        for term, start in (
            (dot(dsc, q, NN), at),
            (dot(wc, g, NN), features + at),
        ):
            begin = 0
            for ref in term_refs:
                amount = ref.shape[0]
                ref[:, start : start + HD] = term[begin : begin + amount].astype(
                    jnp.bfloat16
                )
                begin += amount


def window_kernel(
    counts, valid_ref, q_ref, k_ref, g_ref, dsw_ref, ww_ref, dsc_ref, *refs
):
    coarse = refs[: counts[0]]
    dq_ref, dk_ref, dv_ref = refs[counts[0] :]
    length, features = q_ref.shape
    valid = valid_ref[0, 0]
    live = lax.broadcasted_iota(jnp.int32, (length, HD), 0) % SPAN < valid
    first = lax.broadcasted_iota(jnp.int32, (WIN, PAIR), 1) < WIN
    zero = jnp.zeros((WIN, PAIR), jnp.bfloat16)

    def split(x):
        return jnp.concatenate(
            [jnp.where(first, x, zero), jnp.where(first, zero, x)], axis=0
        )

    for h in range(features // HD):
        at = h * HD
        kc = coarse_rows(coarse, at)
        for p in range(length // PAIR):
            rows = slice(p * PAIR, (p + 1) * PAIR)
            ds = split(dsw_ref[h, :, rows])
            w = split(ww_ref[h, :, rows])
            g = jnp.where(live[rows], g_ref[rows, at : at + HD], 0)
            dk_ref[rows, at : at + HD] = dot(ds, q_ref[rows, at : at + HD], NN)
            dv_ref[rows, at : at + HD] = dot(w, g, NN)
            keys = jnp.concatenate([k_ref[rows, at : at + HD], kc], axis=0)
            all_ds = jnp.concatenate([ds, dsc_ref[h, :, rows]], axis=0)
            dq_ref[rows, at : at + HD] = dot(all_ds, keys, TN).astype(jnp.bfloat16)


def spread_kernel(
    counts, valid_ref, frame_ref, time_ref, dk_ref, dv_ref, *refs
):
    f_refs = refs[: counts[0]]
    t_refs = refs[counts[0] : counts[0] + counts[1]]
    kg_ref, vg_ref = refs[counts[0] + counts[1] :]
    length, features = dk_ref.shape
    member = member_rows(valid_ref[0, 0], frame_ref[...], time_ref[...], length)
    share = 1.0 / jnp.maximum(jnp.sum(member, axis=1, keepdims=True), 1.0)
    both = jnp.concatenate([member, member], axis=0).astype(jnp.bfloat16)
    for out, grad, begin in ((kg_ref, dk_ref, 0), (vg_ref, dv_ref, features)):
        part = slice(begin, begin + features)
        f = functools.reduce(
            lambda a, b: a + b, [r[:, part].astype(jnp.float32) for r in f_refs]
        )
        t = functools.reduce(
            lambda a, b: a + b, [r[:, part].astype(jnp.float32) for r in t_refs]
        )
        pad = jnp.zeros((8 - KT, features), jnp.float32)
        grads = jnp.concatenate([f, t, pad], axis=0) * share
        high = grads.astype(jnp.bfloat16)
        low = (grads - high.astype(jnp.float32)).astype(jnp.bfloat16)
        terms = jnp.concatenate([high.astype(jnp.float32), low.astype(jnp.float32)], 0)
        back = dot(both, terms.astype(jnp.bfloat16), TN)
        out[...] = (grad[...] + back).astype(jnp.bfloat16)


def swap(x, axis, size, mask):
    return lax.ppermute(x, axis, [(i, i ^ mask) for i in range(size)])


def body(tm, space, query, key_in, value_in, grad_out, frame_ids, time_ids, tile_valid):
    length, features = query.shape
    heads = features // HD
    valid = tile_valid.reshape(1, 1)
    frame = frame_ids.reshape(1, length)
    time = time_ids.reshape(1, length)
    bf16, f32 = jnp.bfloat16, jnp.float32
    shape = jax.ShapeDtypeStruct
    size = length * features

    own_f, own_t = call(
        pool_kernel,
        [shape((KF, 2 * features), bf16), shape((KT, 2 * features), bf16)],
        [valid, frame, time, key_in, value_in],
        4 * size * (KF + KT),
        4 * size,
    )

    have_t = own_t
    mask = 1
    while mask < space:
        got = swap(have_t, "space", space, mask)
        mask *= 2
        if mask < space:
            have_t = jnp.concatenate([have_t, got], axis=0)
    time_parts = [have_t, got]
    from_1 = swap(own_f, "tm", tm, 1)
    from_2 = swap(own_f, "tm", tm, 2)
    from_3 = swap(from_2, "tm", tm, 1)
    coarse = [own_f, from_2, from_1, from_3] + time_parts
    total = tm * KF + space * KT

    half = space * KT // 2
    outs = [
        shape((heads, WIN, length), bf16),
        shape((heads, WIN, length), bf16),
        shape((heads, total, length), bf16),
        shape((2 * KF, 2 * features), bf16),
        shape((2 * KF, 2 * features), bf16),
        shape((half, 2 * features), bf16),
        shape((half, 2 * features), bf16),
    ]
    dsw, ww, dsc, f_keep, f_send, t_keep, t_send = call(
        functools.partial(weigh_kernel, (len(coarse),)),
        outs,
        [valid, query, key_in, value_in, grad_out] + coarse,
        4 * size * (PAIR + total) + 4 * size * total,
        8 * size,
    )

    mask = space // 2
    while True:
        got_t = swap(t_send, "space", space, mask)
        if mask == 1:
            break
        summed = (t_keep.astype(f32) + got_t.astype(f32)).astype(bf16)
        amount = summed.shape[0] // 2
        t_keep, t_send = summed[:amount], summed[amount:]
        mask //= 2
    got_f = swap(f_send, "tm", tm, 1)
    summed = (f_keep.astype(f32) + got_f.astype(f32)).astype(bf16)
    f_keep, f_send = summed[:KF], summed[KF:]
    got_f = swap(f_send, "tm", tm, 2)

    query_grad, dk, dv = call(
        functools.partial(window_kernel, (len(coarse),)),
        [
            shape((length, features), bf16),
            shape((length, features), f32),
            shape((length, features), f32),
        ],
        [valid, query, key_in, grad_out, dsw, ww, dsc] + coarse,
        2 * size * (PAIR + total) + 4 * size * PAIR,
        20 * size,
    )
    key_grad, value_grad = call(
        functools.partial(spread_kernel, (2, 2)),
        [shape((length, features), bf16), shape((length, features), bf16)],
        [valid, frame, time, dk, dv, f_keep, got_f, t_keep, got_t],
        8 * size * (KF + KT),
        12 * size,
    )
    return query_grad, key_grad, value_grad


def solution(mesh):
    tm, space = mesh.shape["tm"], mesh.shape["space"]
    rows = P(("groups", "tm", "space"), None)
    ids = P(("groups", "tm", "space"))
    return jax.shard_map(
        functools.partial(body, tm, space),
        mesh=mesh,
        in_specs=(rows, rows, rows, rows, ids, ids, P(("groups", "tm"), "space")),
        out_specs=(rows, rows, rows),
        check_vma=False,
    )
```

```python
import functools
import math

import jax
import jax.numpy as jnp
from jax import lax
from jax.experimental import pallas as pl
from jax.experimental.pallas import tpu as pltpu
from jax.sharding import PartitionSpec as P

HD = 128
WIN = 64
WIN_FRAME = 4
KF = 16
KT = 4
PAIR = 2 * WIN
SPAN = WIN_FRAME * WIN
ROWS = KF + 8
CHUNK = 512

MASK_FILL = -1e30
FACTOR = HD ** (-0.5)
SCALE = FACTOR * math.log2(math.e)
LIMIT = 16 * 1024 * 1024
LOAD_LIMIT = 55000 * 1024
JOIN_FLOPS = 10**9

VMEM = pl.BlockSpec(memory_space=pltpu.VMEM)
HBM = pl.BlockSpec(memory_space=pltpu.HBM)
ANY = pl.BlockSpec(memory_space=pl.ANY)

NT = ((1,), (1,))
NN = ((1,), (0,))
TN = ((0,), (0,))


def dot(a, b, dims):
    return lax.dot_general(a, b, (dims, ((), ())), preferred_element_type=jnp.float32)


def call(kernel, outs, ins, flops, moved, scratch=(), out_specs=None, limit=LIMIT):
    return pl.pallas_call(
        kernel,
        out_shape=outs,
        in_specs=[spec for _, spec in ins],
        out_specs=out_specs or [VMEM] * len(outs),
        scratch_shapes=list(scratch),
        compiler_params=pltpu.CompilerParams(vmem_limit_bytes=limit),
        cost_estimate=pl.CostEstimate(
            flops=flops, bytes_accessed=moved, transcendentals=0
        ),
    )(*[array for array, _ in ins])


def load_kernel(
    code_ref, k_hbm, v_hbm, t_ref, f_ref, member_ref, valid_ref, k_ref, v_ref, sems
):
    copies = [
        pltpu.make_async_copy(k_hbm, k_ref, sems.at[0]),
        pltpu.make_async_copy(v_hbm, v_ref, sems.at[1]),
    ]
    for copy in copies:
        copy.start()
    length, features = k_ref.shape
    code = code_ref[...]
    label = lax.broadcasted_iota(jnp.int32, (ROWS, length), 0)
    ids = jnp.where(label < KF, code // KT, code % KT + KF)
    member = jnp.where((ids == label) & (code >= 0), 1.0, 0.0)
    member_ref[...] = member
    count = jnp.sum(member[:KF], axis=0, keepdims=True)
    count = jnp.sum(count, axis=1, keepdims=True) * (SPAN / length)
    valid_ref[...] = jnp.broadcast_to(count, valid_ref.shape)
    share = 1.0 / jnp.maximum(jnp.sum(member, axis=1, keepdims=True), 1.0)
    table = member.astype(jnp.bfloat16)
    for copy, ref, at in ((copies[0], k_ref, 0), (copies[1], v_ref, features)):
        copy.wait()
        pooled = dot(table, ref[...], NN) * share
        f_ref[:, at : at + features] = pooled[:KF].astype(jnp.bfloat16)
        t_ref[:, at : at + features] = pooled[KF : KF + KT].astype(jnp.bfloat16)


def join_kernel(a_ref, b_ref, out_ref):
    parts = [a_ref[...].astype(jnp.float32), b_ref[...].astype(jnp.float32)]
    out_ref[...] = jnp.concatenate(parts, axis=0).astype(jnp.bfloat16)


def window_kernel(
    valid_ref,
    q_ref,
    raw_ref,
    k_ref,
    v_ref,
    after_ref,
    g_ref,
    e_ref,
    d_ref,
    top_ref,
    sum_ref,
    dot_ref,
):
    del after_ref
    length, features = q_ref.shape
    valid = valid_ref[:1].astype(jnp.int32)
    live = lax.broadcasted_iota(jnp.int32, (length, HD), 0) % SPAN < valid
    lane = lax.broadcasted_iota(jnp.int32, (WIN, PAIR), 1)
    row = lax.broadcasted_iota(jnp.int32, (WIN, PAIR), 0)
    first = lane < WIN
    place = row + jnp.where(first, 0, WIN)
    for h in range(features // HD):
        at = slice(h * HD, (h + 1) * HD)
        g = jnp.where(live, raw_ref[:, at], 0)
        g_ref[:, at] = g
        for p in range(length // PAIR):
            rows = slice(p * PAIR, (p + 1) * PAIR)
            s = dot(k_ref[rows, at], q_ref[rows, at], NT)
            d = dot(v_ref[rows, at], g[rows], NT)
            s = jnp.where(first, s[:WIN], s[WIN:])
            s = jnp.where((place + p * PAIR) % SPAN < valid, s, MASK_FILL)
            d = jnp.where(first, d[:WIN], d[WIN:])
            top = jnp.max(s, axis=0, keepdims=True)
            e = jnp.exp2((s - top) * SCALE)
            e_ref[h, :, rows] = e
            d_ref[h, :, rows] = d
            top_ref[h : h + 1, rows] = top
            sum_ref[h : h + 1, rows] = jnp.sum(e, axis=0, keepdims=True)
            dot_ref[h : h + 1, rows] = jnp.sum(e * d, axis=0, keepdims=True)


def coarse_rows(refs, at):
    parts = [r[:, at : at + HD].astype(jnp.float32) for r in refs]
    return jnp.concatenate(parts, axis=0).astype(jnp.bfloat16)


def coarse_kernel(parts, q_ref, g_ref, top_ref, sum_ref, dot_ref, *refs):
    coarse = refs[:parts]
    ds_ref, weight_ref, delta_ref = refs[parts : parts + 3]
    term_refs = refs[parts + 3 :]
    features = q_ref.shape[1]
    for h in range(features // HD):
        at = h * HD
        row = slice(h, h + 1)
        q = q_ref[:, at : at + HD]
        g = g_ref[:, at : at + HD]
        s = dot(coarse_rows(coarse, at), q, NT)
        d = dot(coarse_rows(coarse, features + at), g, NT)
        window_top = top_ref[row]
        top = jnp.maximum(window_top, jnp.max(s, axis=0, keepdims=True))
        shrink = jnp.exp2((window_top - top) * SCALE)
        e = jnp.exp2((s - top) * SCALE)
        inv = 1.0 / (sum_ref[row] * shrink + jnp.sum(e, axis=0, keepdims=True))
        delta = (dot_ref[row] * shrink + jnp.sum(e * d, axis=0, keepdims=True)) * inv
        weight_ref[row] = shrink * inv
        delta_ref[row] = delta
        w = e * inv
        ds = ((FACTOR * w) * (d - delta)).astype(jnp.bfloat16)
        ds_ref[h] = ds
        for term, start in (
            (dot(ds, q, NN), at),
            (dot(w.astype(jnp.bfloat16), g, NN), features + at),
        ):
            begin = 0
            for ref in term_refs:
                end = begin + ref.shape[0]
                ref[:, start : start + HD] = term[begin:end].astype(jnp.bfloat16)
                begin = end


def local_kernel(
    q_ref, g_ref, e_ref, d_ref, weight_ref, delta_ref, ds_ref, dk_ref, dv_ref
):
    length, features = q_ref.shape
    first = lax.broadcasted_iota(jnp.int32, (WIN, PAIR), 1) < WIN

    def split(x):
        return jnp.concatenate(
            [jnp.where(first, x, 0.0), jnp.where(first, 0.0, x)], axis=0
        ).astype(jnp.bfloat16)

    for h in range(features // HD):
        at = slice(h * HD, (h + 1) * HD)
        for p in range(length // PAIR):
            rows = slice(p * PAIR, (p + 1) * PAIR)
            w = e_ref[h, :, rows] * weight_ref[h : h + 1, rows]
            ds = (FACTOR * w) * (d_ref[h, :, rows] - delta_ref[h : h + 1, rows])
            ds = split(ds)
            ds_ref[h, :, rows] = ds
            dk_ref[rows, at] = dot(ds, q_ref[rows, at], NN)
            dv_ref[rows, at] = dot(split(w), g_ref[rows, at], NN)


def query_kernel(parts, k_ref, ds_ref, dsc_ref, *refs):
    coarse = refs[:parts]
    dq_ref = refs[parts]
    length, features = k_ref.shape
    for h in range(features // HD):
        at = h * HD
        kc = coarse_rows(coarse, at)
        for p in range(length // PAIR):
            rows = slice(p * PAIR, (p + 1) * PAIR)
            keys = jnp.concatenate([k_ref[rows, at : at + HD], kc], axis=0)
            ds = jnp.concatenate([ds_ref[h, :, rows], dsc_ref[h, :, rows]], axis=0)
            dq_ref[rows, at : at + HD] = dot(ds, keys, TN).astype(jnp.bfloat16)


def spread_kernel(
    member_ref,
    dk_ref,
    dv_ref,
    f1_ref,
    f2_ref,
    t1_ref,
    t2_ref,
    kg_hbm,
    vg_hbm,
    kg_ref,
    vg_ref,
    sems,
):
    features = dk_ref.shape[1]
    member = member_ref[...]
    share = 1.0 / jnp.maximum(jnp.sum(member, axis=1, keepdims=True), 1.0)
    both = jnp.concatenate([member, member], axis=0).astype(jnp.bfloat16)
    pad = jnp.zeros((ROWS - KF - KT, CHUNK), jnp.float32)
    copies = []
    for grad, ref, target, begin in (
        (dk_ref, kg_ref, kg_hbm, 0),
        (dv_ref, vg_ref, vg_hbm, features),
    ):
        for start in range(0, features, CHUNK):
            part = slice(begin + start, begin + start + CHUNK)
            here = slice(start, start + CHUNK)
            f = f1_ref[:, part].astype(jnp.float32) + f2_ref[:, part].astype(
                jnp.float32
            )
            t = t1_ref[:, part].astype(jnp.float32) + t2_ref[:, part].astype(
                jnp.float32
            )
            grads = jnp.concatenate([f, t, pad], axis=0) * share
            high = grads.astype(jnp.bfloat16).astype(jnp.float32)
            terms = jnp.concatenate([high, grads - high], axis=0)
            back = dot(both, terms.astype(jnp.bfloat16), TN)
            ref[:, here] = (grad[:, here] + back).astype(jnp.bfloat16)
            copy = pltpu.make_async_copy(
                ref.at[:, here], target.at[:, here], sems.at[len(copies)]
            )
            copy.start()
            copies.append(copy)
    for copy in copies:
        copy.wait()


def swap(x, axis, size, mask):
    return lax.ppermute(x, axis, [(i, i ^ mask) for i in range(size)])


def add(a, b):
    return (a.astype(jnp.float32) + b.astype(jnp.float32)).astype(jnp.bfloat16)


def body(tm, space, query, key_in, value_in, grad_out, frame_ids, time_ids, tile_valid):
    length, features = query.shape
    heads = features // HD
    live = lax.iota(jnp.int32, length) % SPAN < tile_valid.reshape(())
    code = jnp.where(live, frame_ids * KT + time_ids, -1).reshape(1, length)
    bf16, f32 = jnp.bfloat16, jnp.float32
    shape = jax.ShapeDtypeStruct
    size = length * features
    block = shape((length, features), bf16)
    sums = shape((length, features), f32)
    stat = shape((heads, length), f32)

    own_t, own_f, member, valid = call(
        load_kernel,
        [
            shape((KT, 2 * features), bf16),
            shape((KF, 2 * features), bf16),
            shape((ROWS, length), f32),
            shape((8, PAIR), f32),
        ],
        [(code, VMEM), (key_in, HBM), (value_in, HBM)],
        4 * size * ROWS,
        4 * size,
        [
            pltpu.VMEM((length, features), bf16),
            pltpu.VMEM((length, features), bf16),
            pltpu.SemaphoreType.DMA((2,)),
        ],
        limit=LOAD_LIMIT,
    )
    masks = [space >> (i + 1) for i in range(space.bit_length() - 1)]
    have_t = own_t
    for mask in masks[:-1]:
        (have_t,) = call(
            join_kernel,
            [shape((2 * have_t.shape[0], 2 * features), bf16)],
            [(have_t, VMEM), (swap(have_t, "space", space, mask), VMEM)],
            JOIN_FLOPS,
            0,
        )
    got_t = swap(have_t, "space", space, masks[-1])
    from_2 = swap(own_f, "tm", tm, 2)
    from_1 = swap(own_f, "tm", tm, 1)
    from_3 = swap(from_2, "tm", tm, 1)
    coarse = [own_f, from_2, from_1, from_3, jnp.concatenate([have_t, got_t], axis=0)]
    total = tm * KF + space * KT
    coarse_in = [(x, VMEM) for x in coarse]

    g, e, d, top, window_sum, window_dot = call(
        window_kernel,
        [
            block,
            shape((heads, WIN, length), f32),
            shape((heads, WIN, length), f32),
            stat,
            stat,
            stat,
        ],
        [
            (valid, VMEM),
            (query, VMEM),
            (grad_out, VMEM),
            (key_in, VMEM),
            (value_in, VMEM),
            (have_t, ANY),
        ],
        4 * size * PAIR,
        16 * size,
    )

    half = shape((space * KT // 2, 2 * features), bf16)
    pair = shape((2 * KF, 2 * features), bf16)
    dsc, weight, delta, f_keep, f_send, t_keep, t_send = call(
        functools.partial(coarse_kernel, len(coarse)),
        [shape((heads, total, length), bf16), stat, stat, pair, pair, half, half],
        [(x, VMEM) for x in (query, g, top, window_sum, window_dot)] + coarse_in,
        8 * size * total,
        8 * size,
    )

    for mask in masks[:0:-1]:
        summed = add(t_keep, swap(t_send, "space", space, mask))
        t_keep, t_send = jnp.split(summed, 2)
    got_t = swap(t_send, "space", space, masks[0])
    summed = add(f_keep, swap(f_send, "tm", tm, 1))
    f_keep, f_send = summed[:KF], summed[KF:]
    got_f = swap(f_send, "tm", tm, 2)

    ds, dk, dv = call(
        local_kernel,
        [shape((heads, PAIR, length), bf16), sums, sums],
        [(x, VMEM) for x in (query, g, e, d, weight, delta)],
        4 * size * PAIR,
        16 * size,
    )
    (query_grad,) = call(
        functools.partial(query_kernel, len(coarse)),
        [block],
        [(x, VMEM) for x in (key_in, ds, dsc)] + coarse_in,
        2 * size * (PAIR + total),
        6 * size,
    )
    chunks = 2 * features // CHUNK
    key_grad, value_grad = call(
        spread_kernel,
        [block, block],
        [(x, VMEM) for x in (member, dk, dv, f_keep, got_f, t_keep, got_t)],
        8 * size * ROWS,
        12 * size,
        [
            pltpu.VMEM((length, features), bf16),
            pltpu.VMEM((length, features), bf16),
            pltpu.SemaphoreType.DMA((chunks,)),
        ],
        [HBM, HBM],
    )
    return query_grad, key_grad, value_grad


def solution(mesh):
    tm, space = mesh.shape["tm"], mesh.shape["space"]
    rows = P(("groups", "tm", "space"), None)
    ids = P(("groups", "tm", "space"))
    return jax.shard_map(
        functools.partial(body, tm, space),
        mesh=mesh,
        in_specs=(rows, rows, rows, rows, ids, ids, P(("groups", "tm"), "space")),
        out_specs=(rows, rows, rows),
        check_vma=False,
    )
```

```python
import functools
import math

import jax
import jax.numpy as jnp
from jax import lax
from jax.experimental import pallas as pl
from jax.experimental.pallas import tpu as pltpu
from jax.sharding import PartitionSpec as P

HD = 128
WIN = 64
WIN_FRAME = 4
KF = 16
KT = 4
PAIR = 2 * WIN
SPAN = WIN_FRAME * WIN
ROWS = KF + 8
CHUNK = 512

MASK_FILL = -1e30
FACTOR = HD ** (-0.5)
SCALE = FACTOR * math.log2(math.e)
LIMIT = 16 * 1024 * 1024
JOIN_FLOPS = 10**9

VMEM = pl.BlockSpec(memory_space=pltpu.VMEM)
HBM = pl.BlockSpec(memory_space=pltpu.HBM)
ANY = pl.BlockSpec(memory_space=pl.ANY)

NT = ((1,), (1,))
NN = ((1,), (0,))
TN = ((0,), (0,))


def dot(a, b, dims):
    return lax.dot_general(a, b, (dims, ((), ())), preferred_element_type=jnp.float32)


def call(kernel, outs, ins, flops, moved, scratch=(), out_specs=None, limit=LIMIT):
    return pl.pallas_call(
        kernel,
        out_shape=outs,
        in_specs=[spec for _, spec in ins],
        out_specs=out_specs or [VMEM] * len(outs),
        scratch_shapes=list(scratch),
        compiler_params=pltpu.CompilerParams(vmem_limit_bytes=limit),
        cost_estimate=pl.CostEstimate(
            flops=flops, bytes_accessed=moved, transcendentals=0
        ),
    )(*[array for array, _ in ins])


def start_kernel(out_ref):
    out_ref[...] = jnp.zeros_like(out_ref)


def pool_kernel(code_ref, k_ref, v_ref, t_ref, f_ref, member_ref, valid_ref):
    length, features = k_ref.shape
    code = code_ref[...]
    label = lax.broadcasted_iota(jnp.int32, (ROWS, length), 0)
    ids = jnp.where(label < KF, code // KT, code % KT + KF)
    member = jnp.where((ids == label) & (code >= 0), 1.0, 0.0)
    member_ref[...] = member
    count = jnp.sum(member[:KF], axis=0, keepdims=True)
    count = jnp.sum(count, axis=1, keepdims=True) * (SPAN / length)
    valid_ref[...] = jnp.broadcast_to(count, valid_ref.shape)
    share = 1.0 / jnp.maximum(jnp.sum(member, axis=1, keepdims=True), 1.0)
    table = member.astype(jnp.bfloat16)
    for ref, at in ((k_ref, 0), (v_ref, features)):
        pooled = dot(table, ref[...], NN) * share
        f_ref[:, at : at + features] = pooled[:KF].astype(jnp.bfloat16)
        t_ref[:, at : at + features] = pooled[KF : KF + KT].astype(jnp.bfloat16)


def join_kernel(a_ref, b_ref, out_ref):
    parts = [a_ref[...].astype(jnp.float32), b_ref[...].astype(jnp.float32)]
    out_ref[...] = jnp.concatenate(parts, axis=0).astype(jnp.bfloat16)


def halve_kernel(a_ref, b_ref, *refs):
    keep_ref, send_ref = refs[-2:]
    total = a_ref[...].astype(jnp.float32) + b_ref[...].astype(jnp.float32)
    amount = keep_ref.shape[0]
    keep_ref[...] = total[:amount].astype(jnp.bfloat16)
    send_ref[...] = total[amount:].astype(jnp.bfloat16)


def window_kernel(
    valid_ref,
    member_ref,
    q_ref,
    raw_ref,
    k_ref,
    v_ref,
    after_ref,
    g_ref,
    e_ref,
    d_ref,
    top_ref,
    sum_ref,
    dot_ref,
    table_ref,
    share_ref,
):
    del after_ref
    length, features = q_ref.shape
    member = member_ref[...]
    share = 1.0 / jnp.maximum(jnp.sum(member, axis=1, keepdims=True), 1.0)
    share_ref[...] = jnp.broadcast_to(share, share_ref.shape)
    blank = jnp.zeros((HD - 2 * ROWS, length), jnp.float32)
    table = jnp.concatenate([member, member, blank], axis=0)
    table_ref[...] = table.T[:, : 2 * ROWS].astype(jnp.bfloat16)
    valid = valid_ref[:1].astype(jnp.int32)
    live = lax.broadcasted_iota(jnp.int32, (length, HD), 0) % SPAN < valid
    lane = lax.broadcasted_iota(jnp.int32, (WIN, PAIR), 1)
    row = lax.broadcasted_iota(jnp.int32, (WIN, PAIR), 0)
    first = lane < WIN
    place = row + jnp.where(first, 0, WIN)
    for h in range(features // HD):
        at = slice(h * HD, (h + 1) * HD)
        g = jnp.where(live, raw_ref[:, at], 0)
        g_ref[:, at] = g
        for p in range(length // PAIR):
            rows = slice(p * PAIR, (p + 1) * PAIR)
            s = dot(k_ref[rows, at], q_ref[rows, at], NT)
            d = dot(v_ref[rows, at], g[rows], NT)
            s = jnp.where(first, s[:WIN], s[WIN:])
            s = jnp.where((place + p * PAIR) % SPAN < valid, s, MASK_FILL)
            d = jnp.where(first, d[:WIN], d[WIN:])
            top = jnp.max(s, axis=0, keepdims=True)
            e = jnp.exp2((s - top) * SCALE)
            e_ref[h, :, rows] = e
            d_ref[h, :, rows] = d
            top_ref[h : h + 1, rows] = top
            sum_ref[h : h + 1, rows] = jnp.sum(e, axis=0, keepdims=True)
            dot_ref[h : h + 1, rows] = jnp.sum(e * d, axis=0, keepdims=True)


def coarse_rows(refs, at):
    parts = [r[:, at : at + HD].astype(jnp.float32) for r in refs]
    return jnp.concatenate(parts, axis=0).astype(jnp.bfloat16)


def coarse_kernel(parts, q_ref, g_ref, top_ref, sum_ref, dot_ref, *refs):
    coarse = refs[:parts]
    ds_ref, weight_ref, delta_ref = refs[parts : parts + 3]
    term_refs = refs[parts + 3 :]
    features = q_ref.shape[1]
    heads = features // HD

    def products(h):
        at = h * HD
        q = q_ref[:, at : at + HD]
        g = g_ref[:, at : at + HD]
        s = dot(coarse_rows(coarse, at), q, NT)
        d = dot(coarse_rows(coarse, features + at), g, NT)
        return q, g, s, d

    def weigh(h, s, d):
        row = slice(h, h + 1)
        window_top = top_ref[row]
        top = jnp.maximum(window_top, jnp.max(s, axis=0, keepdims=True))
        shrink = jnp.exp2((window_top - top) * SCALE)
        e = jnp.exp2((s - top) * SCALE)
        inv = 1.0 / (sum_ref[row] * shrink + jnp.sum(e, axis=0, keepdims=True))
        delta = (dot_ref[row] * shrink + jnp.sum(e * d, axis=0, keepdims=True)) * inv
        weight_ref[row] = shrink * inv
        delta_ref[row] = delta
        w = e * inv
        ds = ((FACTOR * w) * (d - delta)).astype(jnp.bfloat16)
        ds_ref[h] = ds
        return ds, w.astype(jnp.bfloat16)

    def gradients(h, ds, w, q, g):
        at = h * HD
        for term, start in ((dot(ds, q, NN), at), (dot(w, g, NN), features + at)):
            begin = 0
            for ref in term_refs:
                end = begin + ref.shape[0]
                ref[:, start : start + HD] = term[begin:end].astype(jnp.bfloat16)
                begin = end

    ahead, behind = products(0), None
    for h in range(heads):
        q, g, s, d = ahead
        if h + 1 < heads:
            ahead = products(h + 1)
        if behind:
            gradients(*behind)
        ds, w = weigh(h, s, d)
        behind = (h, ds, w, q, g)
    gradients(*behind)


def local_kernel(
    q_ref, g_ref, e_ref, d_ref, weight_ref, delta_ref, ds_ref, dk_ref, dv_ref
):
    length, features = q_ref.shape
    first = lax.broadcasted_iota(jnp.int32, (WIN, PAIR), 1) < WIN

    def split(x):
        return jnp.concatenate(
            [jnp.where(first, x, 0.0), jnp.where(first, 0.0, x)], axis=0
        ).astype(jnp.bfloat16)

    for h in range(features // HD):
        at = slice(h * HD, (h + 1) * HD)
        for p in range(length // PAIR):
            rows = slice(p * PAIR, (p + 1) * PAIR)
            w = e_ref[h, :, rows] * weight_ref[h : h + 1, rows]
            ds = (FACTOR * w) * (d_ref[h, :, rows] - delta_ref[h : h + 1, rows])
            ds = split(ds)
            ds_ref[h, :, rows] = ds
            dk_ref[rows, at] = dot(ds, q_ref[rows, at], NN)
            dv_ref[rows, at] = dot(split(w), g_ref[rows, at], NN)


def query_kernel(parts, k_ref, ds_ref, dsc_ref, *refs):
    coarse = refs[:parts]
    dq_ref = refs[parts]
    length, features = k_ref.shape
    for h in range(features // HD):
        at = h * HD
        kc = coarse_rows(coarse, at)
        for p in range(length // PAIR):
            rows = slice(p * PAIR, (p + 1) * PAIR)
            keys = jnp.concatenate([k_ref[rows, at : at + HD], kc], axis=0)
            ds = jnp.concatenate([ds_ref[h, :, rows], dsc_ref[h, :, rows]], axis=0)
            dq_ref[rows, at : at + HD] = dot(ds, keys, TN).astype(jnp.bfloat16)


def spread_kernel(f_parts, t_parts, table_ref, share_ref, dk_ref, dv_ref, *refs):
    f_refs = refs[:f_parts]
    t_refs = refs[f_parts : f_parts + t_parts]
    kg_hbm, vg_hbm, kg_ref, vg_ref, sems = refs[f_parts + t_parts :]
    features = dk_ref.shape[1]
    table = table_ref[...]
    share = share_ref[:, :1]
    pad = jnp.zeros((ROWS - KF - KT, CHUNK), jnp.float32)

    def back(begin):
        part = slice(begin, begin + CHUNK)
        f, t = (
            functools.reduce(
                lambda a, b: a + b, [r[:, part].astype(jnp.float32) for r in refs]
            )
            for refs in (f_refs, t_refs)
        )
        grads = jnp.concatenate([f, t, pad], axis=0) * share
        high = grads.astype(jnp.bfloat16).astype(jnp.float32)
        terms = jnp.concatenate([high, grads - high], axis=0)
        return dot(table, terms.astype(jnp.bfloat16), NN)

    copies = []
    ahead = back(0)
    for begin in range(0, 2 * features, CHUNK):
        now = ahead
        if begin + CHUNK < 2 * features:
            ahead = back(begin + CHUNK)
        if begin < features:
            grad, ref, target = dk_ref, kg_ref, kg_hbm
        else:
            grad, ref, target = dv_ref, vg_ref, vg_hbm
        here = slice(begin % features, begin % features + CHUNK)
        ref[:, here] = (grad[:, here] + now).astype(jnp.bfloat16)
        copy = pltpu.make_async_copy(
            ref.at[:, here], target.at[:, here], sems.at[len(copies)]
        )
        copy.start()
        copies.append(copy)
    for copy in copies:
        copy.wait()


def swap(x, axis, size, mask):
    return lax.ppermute(x, axis, [(i, i ^ mask) for i in range(size)])


def body(tm, space, query, key_in, value_in, grad_out, frame_ids, time_ids, tile_valid):
    length, features = query.shape
    heads = features // HD
    bf16, f32 = jnp.bfloat16, jnp.float32
    shape = jax.ShapeDtypeStruct
    size = length * features
    block = shape((length, features), bf16)
    sums = shape((length, features), f32)
    stat = shape((heads, length), f32)

    (zero,) = call(start_kernel, [shape((1, length), jnp.int32)], [], JOIN_FLOPS, 0)
    live = lax.iota(jnp.int32, length) % SPAN < tile_valid.reshape(())
    code = jnp.where(live, frame_ids * KT + time_ids, -1).reshape(1, length) + zero
    own_t, own_f, member, valid = call(
        pool_kernel,
        [
            shape((KT, 2 * features), bf16),
            shape((KF, 2 * features), bf16),
            shape((ROWS, length), f32),
            shape((8, PAIR), f32),
        ],
        [(code, VMEM), (key_in, VMEM), (value_in, VMEM)],
        4 * size * ROWS,
        4 * size,
    )

    masks = [space >> (i + 1) for i in range(space.bit_length() - 1)]
    have_t = own_t
    for mask in masks[:-1]:
        (have_t,) = call(
            join_kernel,
            [shape((2 * have_t.shape[0], 2 * features), bf16)],
            [(have_t, VMEM), (swap(have_t, "space", space, mask), VMEM)],
            JOIN_FLOPS,
            0,
        )
    got_t = swap(have_t, "space", space, masks[-1])
    from_2 = swap(own_f, "tm", tm, 2)
    from_1 = swap(own_f, "tm", tm, 1)
    from_3 = swap(from_2, "tm", tm, 1)
    coarse = [own_f, from_2, from_1, from_3, jnp.concatenate([have_t, got_t], axis=0)]
    total = tm * KF + space * KT
    coarse_in = [(x, VMEM) for x in coarse]

    g, e, d, top, window_sum, window_dot, table, share = call(
        window_kernel,
        [
            block,
            shape((heads, WIN, length), f32),
            shape((heads, WIN, length), f32),
            stat,
            stat,
            stat,
            shape((length, 2 * ROWS), bf16),
            shape((ROWS, HD), f32),
        ],
        [
            (valid, VMEM),
            (member, VMEM),
            (query, VMEM),
            (grad_out, VMEM),
            (key_in, VMEM),
            (value_in, VMEM),
            (have_t, ANY),
        ],
        4 * size * PAIR,
        16 * size,
    )

    half = shape((space * KT // 2, 2 * features), bf16)
    pair = shape((2 * KF, 2 * features), bf16)
    dsc, weight, delta, f_keep, f_send, t_keep, t_send = call(
        functools.partial(coarse_kernel, len(coarse)),
        [shape((heads, total, length), bf16), stat, stat, pair, pair, half, half],
        [(x, VMEM) for x in (query, g, top, window_sum, window_dot)] + coarse_in,
        8 * size * total,
        8 * size,
    )

    ds, dk, dv = call(
        local_kernel,
        [shape((heads, PAIR, length), bf16), sums, sums],
        [(x, VMEM) for x in (query, g, e, d, weight, delta)],
        4 * size * PAIR,
        16 * size,
    )
    def halve(keep, got, flops, after=()):
        part = shape((keep.shape[0] // 2, 2 * features), bf16)
        ins = [(keep, VMEM), (got, VMEM)] + [(x, ANY) for x in after]
        return call(halve_kernel, [part, part], ins, flops, 0)

    for mask in masks[:0:-1]:
        t_keep, t_send = halve(
            t_keep, swap(t_send, "space", space, mask), JOIN_FLOPS, [dk]
        )
    got_t = swap(t_send, "space", space, masks[0])
    f_keep, f_send = halve(f_keep, swap(f_send, "tm", tm, 1), 0)
    got_f = swap(f_send, "tm", tm, 2)

    (query_grad,) = call(
        functools.partial(query_kernel, len(coarse)),
        [block],
        [(x, VMEM) for x in (key_in, ds, dsc)] + coarse_in,
        2 * size * (PAIR + total),
        6 * size,
    )
    chunks = 2 * features // CHUNK
    key_grad, value_grad = call(
        functools.partial(spread_kernel, 2, 2),
        [block, block],
        [(x, VMEM) for x in (table, share, dk, dv, f_keep, got_f, t_keep, got_t)],
        8 * size * ROWS,
        12 * size,
        [
            pltpu.VMEM((length, features), bf16),
            pltpu.VMEM((length, features), bf16),
            pltpu.SemaphoreType.DMA((chunks,)),
        ],
        [HBM, HBM],
    )
    return query_grad, key_grad, value_grad


def solution(mesh):
    tm, space = mesh.shape["tm"], mesh.shape["space"]
    rows = P(("groups", "tm", "space"), None)
    ids = P(("groups", "tm", "space"))
    return jax.shard_map(
        functools.partial(body, tm, space),
        mesh=mesh,
        in_specs=(rows, rows, rows, rows, ids, ids, P(("groups", "tm"), "space")),
        out_specs=(rows, rows, rows),
        check_vma=False,
    )
```

```python
import functools
import math

import jax
import jax.numpy as jnp
from jax import lax
from jax.experimental import pallas as pl
from jax.experimental.pallas import tpu as pltpu
from jax.sharding import PartitionSpec as P

HD = 128
WIN = 64
WIN_FRAME = 4
KF = 16
KT = 4
PAIR = 2 * WIN
SPAN = WIN_FRAME * WIN
ROWS = KF + 8
CHUNK = 512

MASK_FILL = -1e30
FACTOR = HD ** (-0.5)
SCALE = FACTOR * math.log2(math.e)
LIMIT = 16 * 1024 * 1024
JOIN_FLOPS = 10**9

VMEM = pl.BlockSpec(memory_space=pltpu.VMEM)
HBM = pl.BlockSpec(memory_space=pltpu.HBM)
ANY = pl.BlockSpec(memory_space=pl.ANY)

NT = ((1,), (1,))
NN = ((1,), (0,))
TN = ((0,), (0,))


def dot(a, b, dims):
    return lax.dot_general(a, b, (dims, ((), ())), preferred_element_type=jnp.float32)


def call(kernel, outs, ins, flops, moved, scratch=(), out_specs=None, limit=LIMIT):
    return pl.pallas_call(
        kernel,
        out_shape=outs,
        in_specs=[spec for _, spec in ins],
        out_specs=out_specs or [VMEM] * len(outs),
        scratch_shapes=list(scratch),
        compiler_params=pltpu.CompilerParams(vmem_limit_bytes=limit),
        cost_estimate=pl.CostEstimate(
            flops=flops, bytes_accessed=moved, transcendentals=0
        ),
    )(*[array for array, _ in ins])


def start_kernel(out_ref):
    out_ref[...] = jnp.zeros_like(out_ref)


def pool_kernel(code_ref, k_ref, v_ref, t_ref, f_ref, member_ref, valid_ref):
    length, features = k_ref.shape
    code = code_ref[...]
    label = lax.broadcasted_iota(jnp.int32, (ROWS, length), 0)
    ids = jnp.where(label < KF, code // KT, code % KT + KF)
    member = jnp.where((ids == label) & (code >= 0), 1.0, 0.0)
    member_ref[...] = member
    count = jnp.sum(member[:KF], axis=0, keepdims=True)
    count = jnp.sum(count, axis=1, keepdims=True) * (SPAN / length)
    valid_ref[...] = jnp.broadcast_to(count, valid_ref.shape)
    share = 1.0 / jnp.maximum(jnp.sum(member, axis=1, keepdims=True), 1.0)
    table = member.astype(jnp.bfloat16)
    for ref, at in ((k_ref, 0), (v_ref, features)):
        pooled = dot(table, ref[...], NN) * share
        f_ref[:, at : at + features] = pooled[:KF].astype(jnp.bfloat16)
        t_ref[:, at : at + features] = pooled[KF : KF + KT].astype(jnp.bfloat16)


def join_kernel(a_ref, b_ref, *refs):
    out_ref = refs[-1]
    parts = [a_ref[...].astype(jnp.float32), b_ref[...].astype(jnp.float32)]
    out_ref[...] = jnp.concatenate(parts, axis=0).astype(jnp.bfloat16)


def halve_kernel(a_ref, b_ref, *refs):
    keep_ref, send_ref = refs[-2:]
    total = a_ref[...].astype(jnp.float32) + b_ref[...].astype(jnp.float32)
    amount = keep_ref.shape[0]
    keep_ref[...] = total[:amount].astype(jnp.bfloat16)
    send_ref[...] = total[amount:].astype(jnp.bfloat16)


def value_kernel(
    valid_ref, member_ref, raw_ref, v_ref, after_ref, g_ref, d_ref, table_ref, share_ref
):
    del after_ref
    length, features = raw_ref.shape
    member = member_ref[...]
    share = 1.0 / jnp.maximum(jnp.sum(member, axis=1, keepdims=True), 1.0)
    share_ref[...] = jnp.broadcast_to(share, share_ref.shape)
    blank = jnp.zeros((HD - 2 * ROWS, length), jnp.float32)
    table = jnp.concatenate([member, member, blank], axis=0)
    table_ref[...] = table.T[:, : 2 * ROWS].astype(jnp.bfloat16)
    valid = valid_ref[:1].astype(jnp.int32)
    live = lax.broadcasted_iota(jnp.int32, (length, HD), 0) % SPAN < valid
    first = lax.broadcasted_iota(jnp.int32, (WIN, PAIR), 1) < WIN
    for h in range(features // HD):
        at = slice(h * HD, (h + 1) * HD)
        g = jnp.where(live, raw_ref[:, at], 0)
        g_ref[:, at] = g
        for p in range(length // PAIR):
            rows = slice(p * PAIR, (p + 1) * PAIR)
            d = dot(v_ref[rows, at], g[rows], NT)
            d_ref[h, :, rows] = jnp.where(first, d[:WIN], d[WIN:])


def window_kernel(
    valid_ref, q_ref, k_ref, d_ref, after_ref, e_ref, top_ref, sum_ref, dot_ref
):
    del after_ref
    length, features = q_ref.shape
    valid = valid_ref[:1].astype(jnp.int32)
    lane = lax.broadcasted_iota(jnp.int32, (WIN, PAIR), 1)
    row = lax.broadcasted_iota(jnp.int32, (WIN, PAIR), 0)
    first = lane < WIN
    place = row + jnp.where(first, 0, WIN)
    steps = [(h, p) for h in range(features // HD) for p in range(length // PAIR)]

    def products(h, p):
        rows = slice(p * PAIR, (p + 1) * PAIR)
        at = slice(h * HD, (h + 1) * HD)
        return dot(k_ref[rows, at], q_ref[rows, at], NT)

    ahead = products(*steps[0])
    for step, (h, p) in enumerate(steps):
        s = ahead
        if step + 1 < len(steps):
            ahead = products(*steps[step + 1])
        rows = slice(p * PAIR, (p + 1) * PAIR)
        s = jnp.where(first, s[:WIN], s[WIN:])
        s = jnp.where((place + p * PAIR) % SPAN < valid, s, MASK_FILL)
        top = jnp.max(s, axis=0, keepdims=True)
        e = jnp.exp2((s - top) * SCALE)
        e_ref[h, :, rows] = e
        top_ref[h : h + 1, rows] = top
        sum_ref[h : h + 1, rows] = jnp.sum(e, axis=0, keepdims=True)
        dot_ref[h : h + 1, rows] = jnp.sum(e * d_ref[h, :, rows], axis=0, keepdims=True)


def coarse_rows(refs, at):
    parts = [r[:, at : at + HD].astype(jnp.float32) for r in refs]
    return jnp.concatenate(parts, axis=0).astype(jnp.bfloat16)


def coarse_kernel(parts, q_ref, g_ref, top_ref, sum_ref, dot_ref, *refs):
    coarse = refs[:parts]
    ds_ref, weight_ref, delta_ref = refs[parts : parts + 3]
    term_refs = refs[parts + 3 :]
    features = q_ref.shape[1]
    heads = features // HD

    def products(h):
        at = h * HD
        q = q_ref[:, at : at + HD]
        g = g_ref[:, at : at + HD]
        s = dot(coarse_rows(coarse, at), q, NT)
        d = dot(coarse_rows(coarse, features + at), g, NT)
        return q, g, s, d

    def weigh(h, s, d):
        row = slice(h, h + 1)
        window_top = top_ref[row]
        top = jnp.maximum(window_top, jnp.max(s, axis=0, keepdims=True))
        shrink = jnp.exp2((window_top - top) * SCALE)
        e = jnp.exp2((s - top) * SCALE)
        inv = 1.0 / (sum_ref[row] * shrink + jnp.sum(e, axis=0, keepdims=True))
        delta = (dot_ref[row] * shrink + jnp.sum(e * d, axis=0, keepdims=True)) * inv
        weight_ref[row] = shrink * inv
        delta_ref[row] = delta
        w = e * inv
        ds = ((FACTOR * w) * (d - delta)).astype(jnp.bfloat16)
        ds_ref[h] = ds
        return ds, w.astype(jnp.bfloat16)

    def gradients(h, ds, w, q, g):
        at = h * HD
        for term, start in ((dot(ds, q, NN), at), (dot(w, g, NN), features + at)):
            begin = 0
            for ref in term_refs:
                end = begin + ref.shape[0]
                ref[:, start : start + HD] = term[begin:end].astype(jnp.bfloat16)
                begin = end

    ahead, behind = products(0), None
    for h in range(heads):
        q, g, s, d = ahead
        if h + 1 < heads:
            ahead = products(h + 1)
        if behind:
            gradients(*behind)
        ds, w = weigh(h, s, d)
        behind = (h, ds, w, q, g)
    gradients(*behind)


def local_kernel(
    q_ref, g_ref, e_ref, d_ref, weight_ref, delta_ref, ds_ref, dk_ref, dv_ref
):
    length, features = q_ref.shape
    first = lax.broadcasted_iota(jnp.int32, (WIN, PAIR), 1) < WIN

    def split(x):
        return jnp.concatenate(
            [jnp.where(first, x, 0.0), jnp.where(first, 0.0, x)], axis=0
        ).astype(jnp.bfloat16)

    for h in range(features // HD):
        at = slice(h * HD, (h + 1) * HD)
        for p in range(length // PAIR):
            rows = slice(p * PAIR, (p + 1) * PAIR)
            w = e_ref[h, :, rows] * weight_ref[h : h + 1, rows]
            ds = (FACTOR * w) * (d_ref[h, :, rows] - delta_ref[h : h + 1, rows])
            ds = split(ds)
            ds_ref[h, :, rows] = ds
            dk_ref[rows, at] = dot(ds, q_ref[rows, at], NN)
            dv_ref[rows, at] = dot(split(w), g_ref[rows, at], NN)


def query_kernel(parts, k_ref, ds_ref, dsc_ref, *refs):
    coarse = refs[:parts]
    dq_ref = refs[parts]
    length, features = k_ref.shape
    for h in range(features // HD):
        at = h * HD
        kc = coarse_rows(coarse, at)
        for p in range(length // PAIR):
            rows = slice(p * PAIR, (p + 1) * PAIR)
            keys = jnp.concatenate([k_ref[rows, at : at + HD], kc], axis=0)
            ds = jnp.concatenate([ds_ref[h, :, rows], dsc_ref[h, :, rows]], axis=0)
            dq_ref[rows, at : at + HD] = dot(ds, keys, TN).astype(jnp.bfloat16)


def spread_kernel(f_parts, t_parts, table_ref, share_ref, dk_ref, dv_ref, *refs):
    f_refs = refs[:f_parts]
    t_refs = refs[f_parts : f_parts + t_parts]
    kg_hbm, vg_hbm, kg_ref, vg_ref, sems = refs[f_parts + t_parts :]
    features = dk_ref.shape[1]
    table = table_ref[...]
    share = share_ref[:, :1]
    pad = jnp.zeros((ROWS - KF - KT, CHUNK), jnp.float32)

    def back(begin):
        part = slice(begin, begin + CHUNK)
        f, t = (
            functools.reduce(
                lambda a, b: a + b, [r[:, part].astype(jnp.float32) for r in refs]
            )
            for refs in (f_refs, t_refs)
        )
        grads = jnp.concatenate([f, t, pad], axis=0) * share
        high = grads.astype(jnp.bfloat16).astype(jnp.float32)
        terms = jnp.concatenate([high, grads - high], axis=0)
        return dot(table, terms.astype(jnp.bfloat16), NN)

    copies = []
    ahead = back(0)
    for begin in range(0, 2 * features, CHUNK):
        now = ahead
        if begin + CHUNK < 2 * features:
            ahead = back(begin + CHUNK)
        if begin < features:
            grad, ref, target = dk_ref, kg_ref, kg_hbm
        else:
            grad, ref, target = dv_ref, vg_ref, vg_hbm
        here = slice(begin % features, begin % features + CHUNK)
        ref[:, here] = (grad[:, here] + now).astype(jnp.bfloat16)
        copy = pltpu.make_async_copy(
            ref.at[:, here], target.at[:, here], sems.at[len(copies)]
        )
        copy.start()
        copies.append(copy)
    for copy in copies:
        copy.wait()


def swap(x, axis, size, mask):
    return lax.ppermute(x, axis, [(i, i ^ mask) for i in range(size)])


def body(tm, space, query, key_in, value_in, grad_out, frame_ids, time_ids, tile_valid):
    length, features = query.shape
    heads = features // HD
    bf16, f32 = jnp.bfloat16, jnp.float32
    shape = jax.ShapeDtypeStruct
    size = length * features
    block = shape((length, features), bf16)
    sums = shape((length, features), f32)
    stat = shape((heads, length), f32)

    (zero,) = call(start_kernel, [shape((1, length), jnp.int32)], [], JOIN_FLOPS, 0)
    live = lax.iota(jnp.int32, length) % SPAN < tile_valid.reshape(())
    code = jnp.where(live, frame_ids * KT + time_ids, -1).reshape(1, length) + zero
    own_t, own_f, member, valid = call(
        pool_kernel,
        [
            shape((KT, 2 * features), bf16),
            shape((KF, 2 * features), bf16),
            shape((ROWS, length), f32),
            shape((8, PAIR), f32),
        ],
        [(code, VMEM), (key_in, VMEM), (value_in, VMEM)],
        4 * size * ROWS,
        4 * size,
    )

    def join(a, b, flops, after=()):
        ins = [(a, VMEM), (b, VMEM)] + [(x, ANY) for x in after]
        both = shape((a.shape[0] + b.shape[0], 2 * features), bf16)
        return call(join_kernel, [both], ins, flops, 0)[0]

    masks = [space >> (i + 1) for i in range(space.bit_length() - 1)]
    have_t = own_t
    for mask in masks[:-1]:
        have_t = join(have_t, swap(have_t, "space", space, mask), JOIN_FLOPS)
    got_t = swap(have_t, "space", space, masks[-1])
    from_2 = swap(own_f, "tm", tm, 2)
    from_1 = swap(own_f, "tm", tm, 1)
    from_3 = swap(from_2, "tm", tm, 1)
    total = tm * KF + space * KT

    wide = shape((heads, WIN, length), f32)
    g, d, table, share = call(
        value_kernel,
        [block, wide, shape((length, 2 * ROWS), bf16), shape((ROWS, HD), f32)],
        [(x, VMEM) for x in (valid, member, grad_out, value_in)] + [(have_t, ANY)],
        2 * size * PAIR,
        8 * size,
    )
    e, top, window_sum, window_dot = call(
        window_kernel,
        [wide, stat, stat, stat],
        [(x, VMEM) for x in (valid, query, key_in, d)] + [(from_2, ANY)],
        2 * size * PAIR,
        8 * size,
    )

    coarse = [own_f, from_2, from_1, from_3, join(have_t, got_t, JOIN_FLOPS, [top])]
    coarse_in = [(x, VMEM) for x in coarse]
    half = shape((space * KT // 2, 2 * features), bf16)
    pair = shape((2 * KF, 2 * features), bf16)
    dsc, weight, delta, f_keep, f_send, t_keep, t_send = call(
        functools.partial(coarse_kernel, len(coarse)),
        [shape((heads, total, length), bf16), stat, stat, pair, pair, half, half],
        [(x, VMEM) for x in (query, g, top, window_sum, window_dot)] + coarse_in,
        8 * size * total,
        8 * size,
    )

    ds, dk, dv = call(
        local_kernel,
        [shape((heads, PAIR, length), bf16), sums, sums],
        [(x, VMEM) for x in (query, g, e, d, weight, delta)],
        4 * size * PAIR,
        16 * size,
    )
    def halve(keep, got, flops, after=()):
        part = shape((keep.shape[0] // 2, 2 * features), bf16)
        ins = [(keep, VMEM), (got, VMEM)] + [(x, ANY) for x in after]
        return call(halve_kernel, [part, part], ins, flops, 0)

    for mask in masks[:0:-1]:
        t_keep, t_send = halve(
            t_keep, swap(t_send, "space", space, mask), JOIN_FLOPS, [dk]
        )
    got_t = swap(t_send, "space", space, masks[0])
    f_keep, f_send = halve(f_keep, swap(f_send, "tm", tm, 1), 0)
    got_f = swap(f_send, "tm", tm, 2)

    (query_grad,) = call(
        functools.partial(query_kernel, len(coarse)),
        [block],
        [(x, VMEM) for x in (key_in, ds, dsc)] + coarse_in,
        2 * size * (PAIR + total),
        6 * size,
    )
    chunks = 2 * features // CHUNK
    key_grad, value_grad = call(
        functools.partial(spread_kernel, 2, 2),
        [block, block],
        [(x, VMEM) for x in (table, share, dk, dv, f_keep, got_f, t_keep, got_t)],
        8 * size * ROWS,
        12 * size,
        [
            pltpu.VMEM((length, features), bf16),
            pltpu.VMEM((length, features), bf16),
            pltpu.SemaphoreType.DMA((chunks,)),
        ],
        [HBM, HBM],
    )
    return query_grad, key_grad, value_grad


def solution(mesh):
    tm, space = mesh.shape["tm"], mesh.shape["space"]
    rows = P(("groups", "tm", "space"), None)
    ids = P(("groups", "tm", "space"))
    return jax.shard_map(
        functools.partial(body, tm, space),
        mesh=mesh,
        in_specs=(rows, rows, rows, rows, ids, ids, P(("groups", "tm"), "space")),
        out_specs=(rows, rows, rows),
        check_vma=False,
    )
```

```python
import functools
import math

import jax
import jax.numpy as jnp
from jax import lax
from jax.experimental import pallas as pl
from jax.experimental.pallas import tpu as pltpu
from jax.sharding import PartitionSpec as P

HD = 128
WIN = 64
WIN_FRAME = 4
KF = 16
KT = 4
PAIR = 2 * WIN
SPAN = WIN_FRAME * WIN
ROWS = KF + 8
CHUNK = 512

MASK_FILL = -1e30
FACTOR = HD ** (-0.5)
SCALE = FACTOR * math.log2(math.e)
LIMIT = 16 * 1024 * 1024
JOIN_FLOPS = 10**9

VMEM = pl.BlockSpec(memory_space=pltpu.VMEM)
HBM = pl.BlockSpec(memory_space=pltpu.HBM)
ANY = pl.BlockSpec(memory_space=pl.ANY)

NT = ((1,), (1,))
NN = ((1,), (0,))
TN = ((0,), (0,))


def dot(a, b, dims):
    return lax.dot_general(a, b, (dims, ((), ())), preferred_element_type=jnp.float32)


def call(kernel, outs, ins, flops, moved, scratch=(), out_specs=None, limit=LIMIT):
    return pl.pallas_call(
        kernel,
        out_shape=outs,
        in_specs=[spec for _, spec in ins],
        out_specs=out_specs or [VMEM] * len(outs),
        scratch_shapes=list(scratch),
        compiler_params=pltpu.CompilerParams(vmem_limit_bytes=limit),
        cost_estimate=pl.CostEstimate(
            flops=flops, bytes_accessed=moved, transcendentals=0
        ),
    )(*[array for array, _ in ins])


def start_kernel(out_ref):
    out_ref[...] = jnp.zeros_like(out_ref)


def pool_key_kernel(
    code_ref, k_ref, t_ref, f_ref, member_ref, valid_ref, share_ref
):
    length = k_ref.shape[0]
    code = code_ref[...]
    label = lax.broadcasted_iota(jnp.int32, (ROWS, length), 0)
    ids = jnp.where(label < KF, code // KT, code % KT + KF)
    member = jnp.where((ids == label) & (code >= 0), 1.0, 0.0)
    member_ref[...] = member
    count = jnp.sum(member[:KF], axis=0, keepdims=True)
    count = jnp.sum(count, axis=1, keepdims=True) * (SPAN / length)
    valid_ref[...] = jnp.broadcast_to(count, valid_ref.shape)
    share = 1.0 / jnp.maximum(jnp.sum(member, axis=1, keepdims=True), 1.0)
    share_ref[...] = jnp.broadcast_to(share, share_ref.shape)
    pooled = dot(member.astype(jnp.bfloat16), k_ref[...], NN) * share
    f_ref[...] = pooled[:KF].astype(jnp.bfloat16)
    t_ref[...] = pooled[KF : KF + KT].astype(jnp.bfloat16)


def pool_value_kernel(member_ref, share_ref, tk_ref, fk_ref, v_ref, t_ref, f_ref):
    features = v_ref.shape[1]
    t_ref[:, :features] = tk_ref[...]
    f_ref[:, :features] = fk_ref[...]
    pooled = dot(member_ref[...].astype(jnp.bfloat16), v_ref[...], NN) * share_ref[:, :1]
    f_ref[:, features:] = pooled[:KF].astype(jnp.bfloat16)
    t_ref[:, features:] = pooled[KF : KF + KT].astype(jnp.bfloat16)


def join_kernel(a_ref, b_ref, *refs):
    out_ref = refs[-1]
    parts = [a_ref[...].astype(jnp.float32), b_ref[...].astype(jnp.float32)]
    out_ref[...] = jnp.concatenate(parts, axis=0).astype(jnp.bfloat16)


def halve_kernel(a_ref, b_ref, *refs):
    keep_ref, send_ref = refs[-2:]
    total = a_ref[...].astype(jnp.float32) + b_ref[...].astype(jnp.float32)
    amount = keep_ref.shape[0]
    keep_ref[...] = total[:amount].astype(jnp.bfloat16)
    send_ref[...] = total[amount:].astype(jnp.bfloat16)


def value_kernel(
    valid_ref, member_ref, raw_ref, v_ref, after_ref, g_ref, d_ref, table_ref
):
    del after_ref
    length, features = raw_ref.shape
    member = member_ref[...]
    blank = jnp.zeros((HD - 2 * ROWS, length), jnp.float32)
    table = jnp.concatenate([member, member, blank], axis=0)
    table_ref[...] = table.T[:, : 2 * ROWS].astype(jnp.bfloat16)
    valid = valid_ref[:1].astype(jnp.int32)
    live = lax.broadcasted_iota(jnp.int32, (length, HD), 0) % SPAN < valid
    first = lax.broadcasted_iota(jnp.int32, (WIN, PAIR), 1) < WIN
    for h in range(features // HD):
        at = slice(h * HD, (h + 1) * HD)
        g = jnp.where(live, raw_ref[:, at], 0)
        g_ref[:, at] = g
        for p in range(length // PAIR):
            rows = slice(p * PAIR, (p + 1) * PAIR)
            d = dot(v_ref[rows, at], g[rows], NT)
            d_ref[h, :, rows] = jnp.where(first, d[:WIN], d[WIN:])


def window_kernel(
    valid_ref, q_ref, k_ref, d_ref, after_ref, e_ref, top_ref, sum_ref, dot_ref
):
    del after_ref
    length, features = q_ref.shape
    valid = valid_ref[:1].astype(jnp.int32)
    lane = lax.broadcasted_iota(jnp.int32, (WIN, PAIR), 1)
    row = lax.broadcasted_iota(jnp.int32, (WIN, PAIR), 0)
    first = lane < WIN
    place = row + jnp.where(first, 0, WIN)
    steps = [(h, p) for h in range(features // HD) for p in range(length // PAIR)]

    def products(h, p):
        rows = slice(p * PAIR, (p + 1) * PAIR)
        at = slice(h * HD, (h + 1) * HD)
        return dot(k_ref[rows, at], q_ref[rows, at], NT)

    ahead = products(*steps[0])
    for step, (h, p) in enumerate(steps):
        s = ahead
        if step + 1 < len(steps):
            ahead = products(*steps[step + 1])
        rows = slice(p * PAIR, (p + 1) * PAIR)
        s = jnp.where(first, s[:WIN], s[WIN:])
        s = jnp.where((place + p * PAIR) % SPAN < valid, s, MASK_FILL)
        top = jnp.max(s, axis=0, keepdims=True)
        e = jnp.exp2((s - top) * SCALE)
        e_ref[h, :, rows] = e
        top_ref[h : h + 1, rows] = top
        sum_ref[h : h + 1, rows] = jnp.sum(e, axis=0, keepdims=True)
        dot_ref[h : h + 1, rows] = jnp.sum(e * d_ref[h, :, rows], axis=0, keepdims=True)


def coarse_rows(refs, at):
    parts = [r[:, at : at + HD].astype(jnp.float32) for r in refs]
    return jnp.concatenate(parts, axis=0).astype(jnp.bfloat16)


def coarse_kernel(parts, q_ref, g_ref, top_ref, sum_ref, dot_ref, *refs):
    coarse = refs[:parts]
    ds_ref, weight_ref, delta_ref = refs[parts : parts + 3]
    term_refs = refs[parts + 3 :]
    features = q_ref.shape[1]
    heads = features // HD

    def products(h):
        at = h * HD
        q = q_ref[:, at : at + HD]
        g = g_ref[:, at : at + HD]
        s = dot(coarse_rows(coarse, at), q, NT)
        d = dot(coarse_rows(coarse, features + at), g, NT)
        return q, g, s, d

    def weigh(h, s, d):
        row = slice(h, h + 1)
        window_top = top_ref[row]
        top = jnp.maximum(window_top, jnp.max(s, axis=0, keepdims=True))
        shrink = jnp.exp2((window_top - top) * SCALE)
        e = jnp.exp2((s - top) * SCALE)
        inv = 1.0 / (sum_ref[row] * shrink + jnp.sum(e, axis=0, keepdims=True))
        delta = (dot_ref[row] * shrink + jnp.sum(e * d, axis=0, keepdims=True)) * inv
        weight_ref[row] = shrink * inv
        delta_ref[row] = delta
        w = e * inv
        ds = ((FACTOR * w) * (d - delta)).astype(jnp.bfloat16)
        ds_ref[h] = ds
        return ds, w.astype(jnp.bfloat16)

    def gradients(h, ds, w, q, g):
        at = h * HD
        for term, start in ((dot(ds, q, NN), at), (dot(w, g, NN), features + at)):
            begin = 0
            for ref in term_refs:
                end = begin + ref.shape[0]
                ref[:, start : start + HD] = term[begin:end].astype(jnp.bfloat16)
                begin = end

    ahead, behind = [products(h) for h in range(min(2, heads))], None
    for h in range(heads):
        q, g, s, d = ahead.pop(0)
        if h + 2 < heads:
            ahead.append(products(h + 2))
        if behind:
            gradients(*behind)
        ds, w = weigh(h, s, d)
        behind = (h, ds, w, q, g)
    gradients(*behind)


def local_kernel(
    q_ref, g_ref, e_ref, d_ref, weight_ref, delta_ref, ds_ref, dk_ref, dv_ref
):
    length, features = q_ref.shape
    first = lax.broadcasted_iota(jnp.int32, (WIN, PAIR), 1) < WIN

    def split(x):
        return jnp.concatenate(
            [jnp.where(first, x, 0.0), jnp.where(first, 0.0, x)], axis=0
        ).astype(jnp.bfloat16)

    for h in range(features // HD):
        at = slice(h * HD, (h + 1) * HD)
        for p in range(length // PAIR):
            rows = slice(p * PAIR, (p + 1) * PAIR)
            w = e_ref[h, :, rows] * weight_ref[h : h + 1, rows]
            ds = (FACTOR * w) * (d_ref[h, :, rows] - delta_ref[h : h + 1, rows])
            ds = split(ds)
            ds_ref[h, :, rows] = ds
            dk_ref[rows, at] = dot(ds, q_ref[rows, at], NN)
            dv_ref[rows, at] = dot(split(w), g_ref[rows, at], NN)


def query_kernel(parts, k_ref, ds_ref, dsc_ref, *refs):
    coarse = refs[:parts]
    dq_ref = refs[parts]
    length, features = k_ref.shape
    for h in range(features // HD):
        at = h * HD
        kc = coarse_rows(coarse, at)
        for p in range(length // PAIR):
            rows = slice(p * PAIR, (p + 1) * PAIR)
            keys = jnp.concatenate([k_ref[rows, at : at + HD], kc], axis=0)
            ds = jnp.concatenate([ds_ref[h, :, rows], dsc_ref[h, :, rows]], axis=0)
            dq_ref[rows, at : at + HD] = dot(ds, keys, TN).astype(jnp.bfloat16)


def spread_kernel(f_parts, t_parts, table_ref, share_ref, dk_ref, dv_ref, *refs):
    f_refs = refs[:f_parts]
    t_refs = refs[f_parts : f_parts + t_parts]
    kg_hbm, vg_hbm, kg_ref, vg_ref, sems = refs[f_parts + t_parts :]
    features = dk_ref.shape[1]
    table = table_ref[...]
    share = share_ref[:, :1]
    pad = jnp.zeros((ROWS - KF - KT, CHUNK), jnp.float32)

    def back(begin):
        part = slice(begin, begin + CHUNK)
        f, t = (
            functools.reduce(
                lambda a, b: a + b, [r[:, part].astype(jnp.float32) for r in refs]
            )
            for refs in (f_refs, t_refs)
        )
        grads = jnp.concatenate([f, t, pad], axis=0) * share
        high = grads.astype(jnp.bfloat16).astype(jnp.float32)
        terms = jnp.concatenate([high, grads - high], axis=0)
        return dot(table, terms.astype(jnp.bfloat16), NN)

    copies = []
    ahead = back(0)
    for begin in range(0, 2 * features, CHUNK):
        now = ahead
        if begin + CHUNK < 2 * features:
            ahead = back(begin + CHUNK)
        if begin < features:
            grad, ref, target = dk_ref, kg_ref, kg_hbm
        else:
            grad, ref, target = dv_ref, vg_ref, vg_hbm
        here = slice(begin % features, begin % features + CHUNK)
        ref[:, here] = (grad[:, here] + now).astype(jnp.bfloat16)
        copy = pltpu.make_async_copy(
            ref.at[:, here], target.at[:, here], sems.at[len(copies)]
        )
        copy.start()
        copies.append(copy)
    for copy in copies:
        copy.wait()


def swap(x, axis, size, mask):
    return lax.ppermute(x, axis, [(i, i ^ mask) for i in range(size)])


def body(tm, space, query, key_in, value_in, grad_out, frame_ids, time_ids, tile_valid):
    length, features = query.shape
    heads = features // HD
    bf16, f32 = jnp.bfloat16, jnp.float32
    shape = jax.ShapeDtypeStruct
    size = length * features
    block = shape((length, features), bf16)
    sums = shape((length, features), f32)
    stat = shape((heads, length), f32)

    (zero,) = call(start_kernel, [shape((1, length), jnp.int32)], [], JOIN_FLOPS, 0)
    live = lax.iota(jnp.int32, length) % SPAN < tile_valid.reshape(())
    code = jnp.where(live, frame_ids * KT + time_ids, -1).reshape(1, length) + zero
    tk, fk, member, valid, share = call(
        pool_key_kernel,
        [
            shape((KT, features), bf16),
            shape((KF, features), bf16),
            shape((ROWS, length), f32),
            shape((8, PAIR), f32),
            shape((ROWS, HD), f32),
        ],
        [(x, VMEM) for x in (code, key_in)],
        2 * size * ROWS,
        2 * size,
    )
    own_t, own_f = call(
        pool_value_kernel,
        [shape((KT, 2 * features), bf16), shape((KF, 2 * features), bf16)],
        [(x, VMEM) for x in (member, share, tk, fk, value_in)],
        2 * size * ROWS,
        2 * size,
    )

    def join(a, b, flops, after=()):
        ins = [(a, VMEM), (b, VMEM)] + [(x, ANY) for x in after]
        both = shape((a.shape[0] + b.shape[0], 2 * features), bf16)
        return call(join_kernel, [both], ins, flops, 0)[0]

    masks = [space >> (i + 1) for i in range(space.bit_length() - 1)]
    have_t = own_t
    for mask in masks[:-1]:
        have_t = join(have_t, swap(have_t, "space", space, mask), JOIN_FLOPS)
    got_t = swap(have_t, "space", space, masks[-1])
    from_2 = swap(own_f, "tm", tm, 2)
    from_1 = swap(own_f, "tm", tm, 1)
    from_3 = swap(from_2, "tm", tm, 1)
    total = tm * KF + space * KT

    wide = shape((heads, WIN, length), f32)
    g, d, table = call(
        value_kernel,
        [block, wide, shape((length, 2 * ROWS), bf16)],
        [(x, VMEM) for x in (valid, member, grad_out, value_in)] + [(have_t, ANY)],
        2 * size * PAIR,
        8 * size,
    )
    e, top, window_sum, window_dot = call(
        window_kernel,
        [wide, stat, stat, stat],
        [(x, VMEM) for x in (valid, query, key_in, d)] + [(from_2, ANY)],
        2 * size * PAIR,
        8 * size,
    )

    coarse = [own_f, from_2, from_1, from_3, join(have_t, got_t, JOIN_FLOPS, [top])]
    coarse_in = [(x, VMEM) for x in coarse]
    half = shape((space * KT // 2, 2 * features), bf16)
    pair = shape((2 * KF, 2 * features), bf16)
    dsc, weight, delta, f_keep, f_send, t_keep, t_send = call(
        functools.partial(coarse_kernel, len(coarse)),
        [shape((heads, total, length), bf16), stat, stat, pair, pair, half, half],
        [(x, VMEM) for x in (query, g, top, window_sum, window_dot)] + coarse_in,
        8 * size * total,
        8 * size,
    )

    ds, dk, dv = call(
        local_kernel,
        [shape((heads, PAIR, length), bf16), sums, sums],
        [(x, VMEM) for x in (query, g, e, d, weight, delta)],
        4 * size * PAIR,
        16 * size,
    )
    def halve(keep, got, flops, after=()):
        part = shape((keep.shape[0] // 2, 2 * features), bf16)
        ins = [(keep, VMEM), (got, VMEM)] + [(x, ANY) for x in after]
        return call(halve_kernel, [part, part], ins, flops, 0)

    for mask in masks[:0:-1]:
        t_keep, t_send = halve(
            t_keep, swap(t_send, "space", space, mask), JOIN_FLOPS, [dk]
        )
    got_t = swap(t_send, "space", space, masks[0])
    f_keep, f_send = halve(f_keep, swap(f_send, "tm", tm, 1), 0)
    got_f = swap(f_send, "tm", tm, 2)

    (query_grad,) = call(
        functools.partial(query_kernel, len(coarse)),
        [block],
        [(x, VMEM) for x in (key_in, ds, dsc)] + coarse_in,
        2 * size * (PAIR + total),
        6 * size,
    )
    chunks = 2 * features // CHUNK
    key_grad, value_grad = call(
        functools.partial(spread_kernel, 2, 2),
        [block, block],
        [(x, VMEM) for x in (table, share, dk, dv, f_keep, got_f, t_keep, got_t)],
        8 * size * ROWS,
        12 * size,
        [
            pltpu.VMEM((length, features), bf16),
            pltpu.VMEM((length, features), bf16),
            pltpu.SemaphoreType.DMA((chunks,)),
        ],
        [HBM, HBM],
    )
    return query_grad, key_grad, value_grad


def solution(mesh):
    tm, space = mesh.shape["tm"], mesh.shape["space"]
    rows = P(("groups", "tm", "space"), None)
    ids = P(("groups", "tm", "space"))
    return jax.shard_map(
        functools.partial(body, tm, space),
        mesh=mesh,
        in_specs=(rows, rows, rows, rows, ids, ids, P(("groups", "tm"), "space")),
        out_specs=(rows, rows, rows),
        check_vma=False,
    )
```

```python
import functools
import math

import jax
import jax.numpy as jnp
from jax import lax
from jax.experimental import pallas as pl
from jax.experimental.pallas import tpu as pltpu
from jax.sharding import PartitionSpec as P

HD = 128
WIN = 64
WIN_FRAME = 4
KF = 16
KT = 4
PAIR = 2 * WIN
SPAN = WIN_FRAME * WIN
ROWS = KF + 8
CHUNK = 512
EARLY = 6

MASK_FILL = -1e30
FACTOR = HD ** (-0.5)
SCALE = FACTOR * math.log2(math.e)
LIMIT = 16 * 1024 * 1024
JOIN_FLOPS = 10**9

VMEM = pl.BlockSpec(memory_space=pltpu.VMEM)
HBM = pl.BlockSpec(memory_space=pltpu.HBM)
ANY = pl.BlockSpec(memory_space=pl.ANY)

NT = ((1,), (1,))
NN = ((1,), (0,))
TN = ((0,), (0,))


def dot(a, b, dims):
    return lax.dot_general(a, b, (dims, ((), ())), preferred_element_type=jnp.float32)


def call(kernel, outs, ins, flops, moved, scratch=(), out_specs=None, limit=LIMIT):
    return pl.pallas_call(
        kernel,
        out_shape=outs,
        in_specs=[spec for _, spec in ins],
        out_specs=out_specs or [VMEM] * len(outs),
        scratch_shapes=list(scratch),
        compiler_params=pltpu.CompilerParams(vmem_limit_bytes=limit),
        cost_estimate=pl.CostEstimate(
            flops=flops, bytes_accessed=moved, transcendentals=0
        ),
    )(*[array for array, _ in ins])


def start_kernel(out_ref):
    out_ref[...] = jnp.zeros_like(out_ref)


def pool_key_kernel(
    code_ref, k_ref, t_ref, f_ref, member_ref, valid_ref, share_ref
):
    length = k_ref.shape[0]
    code = code_ref[...]
    label = lax.broadcasted_iota(jnp.int32, (ROWS, length), 0)
    ids = jnp.where(label < KF, code // KT, code % KT + KF)
    member = jnp.where((ids == label) & (code >= 0), 1.0, 0.0)
    member_ref[...] = member
    count = jnp.sum(member[:KF], axis=0, keepdims=True)
    count = jnp.sum(count, axis=1, keepdims=True) * (SPAN / length)
    valid_ref[...] = jnp.broadcast_to(count, valid_ref.shape)
    share = 1.0 / jnp.maximum(jnp.sum(member, axis=1, keepdims=True), 1.0)
    share_ref[...] = jnp.broadcast_to(share, share_ref.shape)
    pooled = dot(member.astype(jnp.bfloat16), k_ref[...], NN) * share
    f_ref[...] = pooled[:KF].astype(jnp.bfloat16)
    t_ref[...] = pooled[KF : KF + KT].astype(jnp.bfloat16)


def pool_value_kernel(member_ref, share_ref, tk_ref, fk_ref, v_ref, t_ref, f_ref):
    features = v_ref.shape[1]
    t_ref[:, :features] = tk_ref[...]
    f_ref[:, :features] = fk_ref[...]
    pooled = dot(member_ref[...].astype(jnp.bfloat16), v_ref[...], NN) * share_ref[:, :1]
    f_ref[:, features:] = pooled[:KF].astype(jnp.bfloat16)
    t_ref[:, features:] = pooled[KF : KF + KT].astype(jnp.bfloat16)


def join_kernel(a_ref, b_ref, *refs):
    out_ref = refs[-1]
    parts = [a_ref[...].astype(jnp.float32), b_ref[...].astype(jnp.float32)]
    out_ref[...] = jnp.concatenate(parts, axis=0).astype(jnp.bfloat16)


def halve_kernel(a_ref, b_ref, *refs):
    keep_ref, send_ref = refs[-2:]
    total = a_ref[...].astype(jnp.float32) + b_ref[...].astype(jnp.float32)
    amount = keep_ref.shape[0]
    keep_ref[...] = total[:amount].astype(jnp.bfloat16)
    send_ref[...] = total[amount:].astype(jnp.bfloat16)


def value_products(h, g_ref, v_ref):
    at = slice(h * HD, (h + 1) * HD)
    first = lax.broadcasted_iota(jnp.int32, (WIN, PAIR), 1) < WIN
    for p in range(v_ref.shape[0] // PAIR):
        rows = slice(p * PAIR, (p + 1) * PAIR)
        d = dot(v_ref[rows, at], g_ref[rows, at], NT)
        yield rows, jnp.where(first, d[:WIN], d[WIN:])


def value_kernel(valid_ref, raw_ref, v_ref, after_ref, g_ref, d_ref):
    del after_ref
    length, features = raw_ref.shape
    valid = valid_ref[:1].astype(jnp.int32)
    live = lax.broadcasted_iota(jnp.int32, (length, HD), 0) % SPAN < valid
    for h in range(features // HD):
        at = slice(h * HD, (h + 1) * HD)
        g_ref[:, at] = jnp.where(live, raw_ref[:, at], 0)
    for h in range(d_ref.shape[0]):
        for rows, d in value_products(h, g_ref, v_ref):
            d_ref[h, :, rows] = d


def window_kernel(
    valid_ref,
    q_ref,
    k_ref,
    g_ref,
    v_ref,
    d_early,
    after_ref,
    d_late,
    e_ref,
    top_ref,
    sum_ref,
    dot_ref,
):
    del after_ref
    length, features = q_ref.shape
    valid = valid_ref[:1].astype(jnp.int32)
    lane = lax.broadcasted_iota(jnp.int32, (WIN, PAIR), 1)
    row = lax.broadcasted_iota(jnp.int32, (WIN, PAIR), 0)
    first = lane < WIN
    place = row + jnp.where(first, 0, WIN)
    early = d_early.shape[0]

    def products(h):
        at = slice(h * HD, (h + 1) * HD)
        if h < early:
            ds = [
                (slice(p * PAIR, (p + 1) * PAIR), d_early[h, :, p * PAIR : (p + 1) * PAIR])
                for p in range(length // PAIR)
            ]
        else:
            ds = list(value_products(h, g_ref, v_ref))
            for rows, d in ds:
                d_late[h - early, :, rows] = d
        return [(rows, dot(k_ref[rows, at], q_ref[rows, at], NT), d) for rows, d in ds]

    heads = features // HD
    ahead = products(0)
    for h in range(heads):
        now = ahead
        if h + 1 < heads:
            ahead = products(h + 1)
        for rows, s, d in now:
            s = jnp.where(first, s[:WIN], s[WIN:])
            s = jnp.where((place + rows.start) % SPAN < valid, s, MASK_FILL)
            top = jnp.max(s, axis=0, keepdims=True)
            e = jnp.exp2((s - top) * SCALE)
            e_ref[h, :, rows] = e
            top_ref[h : h + 1, rows] = top
            sum_ref[h : h + 1, rows] = jnp.sum(e, axis=0, keepdims=True)
            dot_ref[h : h + 1, rows] = jnp.sum(e * d, axis=0, keepdims=True)


def coarse_rows(refs, at):
    parts = [r[:, at : at + HD].astype(jnp.float32) for r in refs]
    return jnp.concatenate(parts, axis=0).astype(jnp.bfloat16)


def coarse_kernel(parts, q_ref, g_ref, top_ref, sum_ref, dot_ref, *refs):
    coarse = refs[:parts]
    ds_ref, weight_ref, delta_ref = refs[parts : parts + 3]
    term_refs = refs[parts + 3 :]
    features = q_ref.shape[1]
    heads = features // HD

    def products(h):
        at = h * HD
        q = q_ref[:, at : at + HD]
        g = g_ref[:, at : at + HD]
        s = dot(coarse_rows(coarse, at), q, NT)
        d = dot(coarse_rows(coarse, features + at), g, NT)
        return q, g, s, d

    def weigh(h, s, d):
        row = slice(h, h + 1)
        window_top = top_ref[row]
        top = jnp.maximum(window_top, jnp.max(s, axis=0, keepdims=True))
        shrink = jnp.exp2((window_top - top) * SCALE)
        e = jnp.exp2((s - top) * SCALE)
        inv = 1.0 / (sum_ref[row] * shrink + jnp.sum(e, axis=0, keepdims=True))
        delta = (dot_ref[row] * shrink + jnp.sum(e * d, axis=0, keepdims=True)) * inv
        weight_ref[row] = shrink * inv
        delta_ref[row] = delta
        w = e * inv
        ds = ((FACTOR * w) * (d - delta)).astype(jnp.bfloat16)
        ds_ref[h] = ds
        return ds, w.astype(jnp.bfloat16)

    def gradients(h, ds, w, q, g):
        at = h * HD
        for term, start in ((dot(ds, q, NN), at), (dot(w, g, NN), features + at)):
            begin = 0
            for ref in term_refs:
                end = begin + ref.shape[0]
                ref[:, start : start + HD] = term[begin:end].astype(jnp.bfloat16)
                begin = end

    ahead, behind = [products(h) for h in range(min(2, heads))], None
    for h in range(heads):
        q, g, s, d = ahead.pop(0)
        if h + 2 < heads:
            ahead.append(products(h + 2))
        if behind:
            gradients(*behind)
        ds, w = weigh(h, s, d)
        behind = (h, ds, w, q, g)
    gradients(*behind)


def local_kernel(
    q_ref, g_ref, e_ref, d_early, d_late, weight_ref, delta_ref, ds_ref, dk_ref, dv_ref
):
    length, features = q_ref.shape
    first = lax.broadcasted_iota(jnp.int32, (WIN, PAIR), 1) < WIN

    def split(x):
        return jnp.concatenate(
            [jnp.where(first, x, 0.0), jnp.where(first, 0.0, x)], axis=0
        ).astype(jnp.bfloat16)

    early = d_early.shape[0]
    for h in range(features // HD):
        at = slice(h * HD, (h + 1) * HD)
        d_ref, i = (d_early, h) if h < early else (d_late, h - early)
        for p in range(length // PAIR):
            rows = slice(p * PAIR, (p + 1) * PAIR)
            w = e_ref[h, :, rows] * weight_ref[h : h + 1, rows]
            ds = (FACTOR * w) * (d_ref[i, :, rows] - delta_ref[h : h + 1, rows])
            ds = split(ds)
            ds_ref[h, :, rows] = ds
            dk_ref[rows, at] = dot(ds, q_ref[rows, at], NN)
            dv_ref[rows, at] = dot(split(w), g_ref[rows, at], NN)


def query_kernel(parts, member_ref, k_ref, ds_ref, dsc_ref, *refs):
    coarse = refs[:parts]
    dq_ref, table_ref = refs[parts:]
    length, features = k_ref.shape
    member = member_ref[...]
    blank = jnp.zeros((HD - 2 * ROWS, length), jnp.float32)
    table = jnp.concatenate([member, member, blank], axis=0)
    table_ref[...] = table.T[:, : 2 * ROWS].astype(jnp.bfloat16)
    for h in range(features // HD):
        at = h * HD
        kc = coarse_rows(coarse, at)
        for p in range(length // PAIR):
            rows = slice(p * PAIR, (p + 1) * PAIR)
            keys = jnp.concatenate([k_ref[rows, at : at + HD], kc], axis=0)
            ds = jnp.concatenate([ds_ref[h, :, rows], dsc_ref[h, :, rows]], axis=0)
            dq_ref[rows, at : at + HD] = dot(ds, keys, TN).astype(jnp.bfloat16)


def spread_kernel(f_parts, t_parts, table_ref, share_ref, dk_ref, dv_ref, *refs):
    f_refs = refs[:f_parts]
    t_refs = refs[f_parts : f_parts + t_parts]
    kg_hbm, vg_hbm, kg_ref, vg_ref, sems = refs[f_parts + t_parts :]
    features = dk_ref.shape[1]
    table = table_ref[...]
    share = share_ref[:, :1]
    pad = jnp.zeros((ROWS - KF - KT, CHUNK), jnp.float32)

    def back(begin):
        part = slice(begin, begin + CHUNK)
        f, t = (
            functools.reduce(
                lambda a, b: a + b, [r[:, part].astype(jnp.float32) for r in refs]
            )
            for refs in (f_refs, t_refs)
        )
        grads = jnp.concatenate([f, t, pad], axis=0) * share
        high = grads.astype(jnp.bfloat16).astype(jnp.float32)
        terms = jnp.concatenate([high, grads - high], axis=0)
        return dot(table, terms.astype(jnp.bfloat16), NN)

    copies = []
    ahead = back(0)
    for begin in range(0, 2 * features, CHUNK):
        now = ahead
        if begin + CHUNK < 2 * features:
            ahead = back(begin + CHUNK)
        if begin < features:
            grad, ref, target = dk_ref, kg_ref, kg_hbm
        else:
            grad, ref, target = dv_ref, vg_ref, vg_hbm
        here = slice(begin % features, begin % features + CHUNK)
        ref[:, here] = (grad[:, here] + now).astype(jnp.bfloat16)
        copy = pltpu.make_async_copy(
            ref.at[:, here], target.at[:, here], sems.at[len(copies)]
        )
        copy.start()
        copies.append(copy)
    for copy in copies:
        copy.wait()


def swap(x, axis, size, mask):
    return lax.ppermute(x, axis, [(i, i ^ mask) for i in range(size)])


def body(tm, space, query, key_in, value_in, grad_out, frame_ids, time_ids, tile_valid):
    length, features = query.shape
    heads = features // HD
    bf16, f32 = jnp.bfloat16, jnp.float32
    shape = jax.ShapeDtypeStruct
    size = length * features
    block = shape((length, features), bf16)
    sums = shape((length, features), f32)
    stat = shape((heads, length), f32)

    (zero,) = call(start_kernel, [shape((1, length), jnp.int32)], [], JOIN_FLOPS, 0)
    live = lax.iota(jnp.int32, length) % SPAN < tile_valid.reshape(())
    code = jnp.where(live, frame_ids * KT + time_ids, -1).reshape(1, length) + zero
    tk, fk, member, valid, share = call(
        pool_key_kernel,
        [
            shape((KT, features), bf16),
            shape((KF, features), bf16),
            shape((ROWS, length), f32),
            shape((8, PAIR), f32),
            shape((ROWS, HD), f32),
        ],
        [(x, VMEM) for x in (code, key_in)],
        2 * size * ROWS,
        2 * size,
    )
    own_t, own_f = call(
        pool_value_kernel,
        [shape((KT, 2 * features), bf16), shape((KF, 2 * features), bf16)],
        [(x, VMEM) for x in (member, share, tk, fk, value_in)],
        2 * size * ROWS,
        2 * size,
    )

    def join(a, b, flops, after=()):
        ins = [(a, VMEM), (b, VMEM)] + [(x, ANY) for x in after]
        both = shape((a.shape[0] + b.shape[0], 2 * features), bf16)
        return call(join_kernel, [both], ins, flops, 0)[0]

    masks = [space >> (i + 1) for i in range(space.bit_length() - 1)]
    have_t = own_t
    for mask in masks[:-1]:
        have_t = join(have_t, swap(have_t, "space", space, mask), JOIN_FLOPS)
    got_t = swap(have_t, "space", space, masks[-1])
    from_2 = swap(own_f, "tm", tm, 2)
    from_1 = swap(own_f, "tm", tm, 1)
    from_3 = swap(from_2, "tm", tm, 1)
    total = tm * KF + space * KT

    wide = shape((heads, WIN, length), f32)
    early = heads * EARLY // 12
    g, d_early = call(
        value_kernel,
        [block, shape((early, WIN, length), f32)],
        [(x, VMEM) for x in (valid, grad_out, value_in)] + [(have_t, ANY)],
        2 * size * PAIR,
        8 * size,
    )
    d_late, e, top, window_sum, window_dot = call(
        window_kernel,
        [shape((heads - early, WIN, length), f32), wide, stat, stat, stat],
        [(x, VMEM) for x in (valid, query, key_in, g, value_in, d_early)] + [(from_2, ANY)],
        2 * size * PAIR,
        8 * size,
    )

    coarse = [own_f, from_2, from_1, from_3, join(have_t, got_t, JOIN_FLOPS, [top])]
    coarse_in = [(x, VMEM) for x in coarse]
    half = shape((space * KT // 2, 2 * features), bf16)
    pair = shape((2 * KF, 2 * features), bf16)
    dsc, weight, delta, f_keep, f_send, t_keep, t_send = call(
        functools.partial(coarse_kernel, len(coarse)),
        [shape((heads, total, length), bf16), stat, stat, pair, pair, half, half],
        [(x, VMEM) for x in (query, g, top, window_sum, window_dot)] + coarse_in,
        8 * size * total,
        8 * size,
    )

    ds, dk, dv = call(
        local_kernel,
        [shape((heads, PAIR, length), bf16), sums, sums],
        [(x, VMEM) for x in (query, g, e, d_early, d_late, weight, delta)],
        4 * size * PAIR,
        16 * size,
    )
    def halve(keep, got, flops, after=()):
        part = shape((keep.shape[0] // 2, 2 * features), bf16)
        ins = [(keep, VMEM), (got, VMEM)] + [(x, ANY) for x in after]
        return call(halve_kernel, [part, part], ins, flops, 0)

    for mask in masks[:0:-1]:
        t_keep, t_send = halve(
            t_keep, swap(t_send, "space", space, mask), 3 * 10**8, [dk]
        )
    got_t = swap(t_send, "space", space, masks[0])
    f_keep, f_send = halve(f_keep, swap(f_send, "tm", tm, 1), 0)
    got_f = swap(f_send, "tm", tm, 2)

    query_grad, table = call(
        functools.partial(query_kernel, len(coarse)),
        [block, shape((length, 2 * ROWS), bf16)],
        [(x, VMEM) for x in (member, key_in, ds, dsc)] + coarse_in,
        2 * size * (PAIR + total),
        6 * size,
    )
    chunks = 2 * features // CHUNK
    key_grad, value_grad = call(
        functools.partial(spread_kernel, 2, 2),
        [block, block],
        [(x, VMEM) for x in (table, share, dk, dv, f_keep, got_f, t_keep, got_t)],
        8 * size * ROWS,
        12 * size,
        [
            pltpu.VMEM((length, features), bf16),
            pltpu.VMEM((length, features), bf16),
            pltpu.SemaphoreType.DMA((chunks,)),
        ],
        [HBM, HBM],
    )
    return query_grad, key_grad, value_grad


def solution(mesh):
    tm, space = mesh.shape["tm"], mesh.shape["space"]
    rows = P(("groups", "tm", "space"), None)
    ids = P(("groups", "tm", "space"))
    return jax.shard_map(
        functools.partial(body, tm, space),
        mesh=mesh,
        in_specs=(rows, rows, rows, rows, ids, ids, P(("groups", "tm"), "space")),
        out_specs=(rows, rows, rows),
        check_vma=False,
    )
```
